256 devices in a mesh: lon: 16 (over x, y_lo, core), lat: 16 (over z, y_hi).
Axes of the slice: x: 4, y: 4 (y_hi: 2, y_lo: 2; y = y_hi * 2 + y_lo), z: 8, core: 2. Of those that a mesh axis runs over, the one named last changes fastest.
Arguments:
- field: float32 [256, 256, 768], P('lat', 'lon'), may hold values from -6 to 6
- w_qkv: bfloat16 [2, 768, 2304], replicated, may hold values from -2 to 2
- w_proj: bfloat16 [2, 768, 768], replicated, may hold values from -0.21875 to 0.21875
- norm_gain: float32 [2, 768], replicated, may hold values from 0.1 to 1.9
- pos_bias: float32 [2, 12, 64, 64], replicated, may hold values from -4 to 4
Outputs:
- blended: float32 [256, 256, 768], P('lat', 'lon')
The draws below stay inside these ranges and needn't reach their ends.
All inputs are finite; a program needn't handle non-finite values.
Results may differ from the reference program's by a relative error of at most 0.0055.
Values may be sent and summed in bfloat16 or wider, within the bound.
A program may use at most 64 MiB of HBM per device.

```python
import jax
import jax.numpy as jnp
from jax import lax

D = 768
HEADS = 12
WINDOW = 8
HEAD_DIM = 64
SHIFT = 4
WIN_TOKENS = 64
NLAT = 256
NLON = 256


def draw_w_qkv(key, part):
    key = jax.random.fold_in(key, 11)
    first = jax.random.fold_in(key, 0)
    base = jax.random.normal(first, (2, D, 3 * D), jnp.float32) * D ** (-0.5)
    base = jnp.clip(base, -2.0, 2.0)
    return base.astype(jnp.bfloat16)


def block_scale(own_key, extent, pieces, smallest, top_value):
    factor_of = 1.0
    for dim, blocks in pieces:
        draws = jax.random.uniform(jax.random.fold_in(jax.random.fold_in(own_key, 6), dim), (blocks,), jnp.float32, smallest / len(pieces), top_value / len(pieces))
        factor_of = factor_of * jnp.repeat(jnp.exp(draws), extent[dim] // blocks).reshape((-1,) + (1,) * (len(extent) - 1 - dim))
    return factor_of


def scatter_about(stream_key, dims, deviation, most, cuts=(), kind=jnp.bfloat16):
    drawn = deviation * jax.random.normal(stream_key, dims, jnp.float32)
    if cuts:
        drawn = drawn * block_scale(stream_key, dims, cuts, -0.22, 0.18)
    return jnp.clip(drawn, -most, most).astype(kind)


def setup_inputs(seed: int = 0) -> dict:
    splits = jax.random.split(jax.random.key(seed), 6)
    return {
        "field": scatter_about(splits[0], (NLAT, NLON, D), 1.0, 6.0, ((0, 16), (1, 16)), jnp.float32),
        "w_qkv": draw_w_qkv(jax.random.fold_in(splits[5], 71), 0),
        "w_proj": scatter_about(splits[2], (2, D, D), D ** -0.5, 0.21875),
        "norm_gain": jnp.clip(1.0 + 0.18 * jax.random.normal(splits[3], (2, D), jnp.float32), 0.1, 1.9),
        "pos_bias": scatter_about(splits[4], (2, HEADS, WIN_TOKENS, WIN_TOKENS), 1.0, 4.0, (), jnp.float32),
    }


def layer_norm(x, gain):
    mean = lax.optimization_barrier(jnp.mean(x, axis=-1, keepdims=True))
    centred = x - mean
    var = lax.optimization_barrier(jnp.mean(centred * centred, axis=-1, keepdims=True))
    return centred * lax.rsqrt(var + 1e-05) * gain

def partition(x):
    return x.reshape(NLAT // WINDOW, WINDOW, NLON // WINDOW, WINDOW, x.shape[-1]).transpose(0, 2, 1, 3, 4).reshape(NLAT // WINDOW, NLON // WINDOW, WIN_TOKENS, x.shape[-1])

def unpartition(y):
    return y.reshape(NLAT // WINDOW, NLON // WINDOW, WINDOW, WINDOW, y.shape[-1]).transpose(0, 2, 1, 3, 4).reshape(NLAT, NLON, y.shape[-1])

def attend(block, groups, weight_qkv, weight_proj, gain, bias):
    count = block.shape[0]
    normed = layer_norm(block, gain).astype(jnp.bfloat16)
    qkv = jnp.dot(normed.reshape(-1, D), weight_qkv, preferred_element_type=jnp.float32).astype(jnp.bfloat16)
    qkv = qkv.reshape(count, WIN_TOKENS, 3, HEADS, HEAD_DIM)
    query = qkv[:, :, 0].astype(jnp.float32)
    keys = qkv[:, :, 1].astype(jnp.float32)
    values = qkv[:, :, 2].astype(jnp.float32)
    scores = jnp.einsum('wqhd,wkhd->whqk', query, keys) * HEAD_DIM ** (-0.5) + bias[None]
    allowed = (groups[:, :, None] == groups[:, None, :])[:, None]
    scores = jnp.where(allowed, scores, -1e+30)
    top = lax.optimization_barrier(jnp.max(scores, axis=-1, keepdims=True))
    expo = jnp.exp(scores - top)
    probs = (expo / lax.optimization_barrier(jnp.sum(expo, axis=-1, keepdims=True))).astype(jnp.bfloat16)
    context = jnp.einsum('whqk,wkhd->wqhd', probs.astype(jnp.float32), values).astype(jnp.bfloat16)
    update = jnp.dot(context.reshape(-1, D), weight_proj, preferred_element_type=jnp.float32)
    return block + update.reshape(count, WIN_TOKENS, D)

def sublayer(field, offset, weight_qkv, weight_proj, gain, bias):
    rolled = jnp.roll(field, (-offset, -offset), (0, 1))
    lat_rows = (jnp.arange(NLAT, dtype=jnp.int32) + offset) % NLAT
    groups = ((lat_rows + offset) // WINDOW).astype(jnp.int32)
    group_grid = jnp.broadcast_to(groups[:, None], (NLAT, NLON))
    wins = partition(rolled)
    group_wins = partition(group_grid[:, :, None])[..., 0]

    def band(item):
        return attend(item[0], item[1], weight_qkv, weight_proj, gain, bias)
    out = lax.map(band, (wins, group_wins))
    return jnp.roll(unpartition(out), (offset, offset), (0, 1))

def reference(field, w_qkv, w_proj, norm_gain, pos_bias):
    state = sublayer(field, 0, w_qkv[0], w_proj[0], norm_gain[0], pos_bias[0])
    return sublayer(state, SHIFT, w_qkv[1], w_proj[1], norm_gain[1], pos_bias[1])
```

```python
import functools

import jax
import jax.numpy as jnp
from jax import lax
from jax.experimental import pallas as pl
from jax.experimental.pallas import tpu as pltpu
from jax.sharding import PartitionSpec as P

D = 768
HEADS = 12
PAIRS = HEADS // 2
WIN = 64
QUAD = 16
F32 = jnp.float32
BF16 = jnp.bfloat16
MESH = pl.DeviceIdType.MESH
NT = (((1,), (1,)), ((), ()))

ROUTES = ((-1, 0), (1, 0), (0, -1), (0, 1), (-1, -1), (-1, 1), (1, -1), (1, 1))


def route_slices(step):
    if step == -1:
        return pl.ds(1, 1), pl.ds(5, 1)
    if step == 1:
        return pl.ds(4, 1), pl.ds(0, 1)
    return pl.ds(1, 4), pl.ds(1, 4)


def layer_norm(x, gain):
    mean = jnp.mean(x, axis=-1, keepdims=True)
    centred = x - mean
    var = jnp.mean(centred * centred, axis=-1, keepdims=True)
    return centred * lax.rsqrt(var + 1e-05) * gain


def lanes_low(shape, axis):
    return lax.broadcasted_iota(jnp.int32, shape, axis) < 64


def attend(qs, ks, vs, biases):
    low = lanes_low((1, 128), 1)
    keep0 = low.astype(F32).astype(BF16)
    keep1 = (1.0 - low.astype(F32)).astype(BF16)
    diag = (lanes_low((128, 128), 0) == lanes_low((128, 128), 1)).astype(F32).astype(BF16)
    scores = []
    for q, k, bias in zip(qs, ks, biases):
        both = jnp.concatenate([k * keep0, k * keep1], axis=0)
        scores.append(lax.dot_general(q, both, NT, preferred_element_type=F32) + bias)
    tops = []
    for s in scores:
        top0 = jnp.max(jnp.where(low, s, -jnp.inf), axis=-1, keepdims=True)
        top1 = jnp.max(jnp.where(low, -jnp.inf, s), axis=-1, keepdims=True)
        tops.append(jnp.where(low, top0, top1))
    expos = [jnp.exp(s - top).astype(BF16) for s, top in zip(scores, tops)]
    outs = []
    for e, v in zip(expos, vs):
        both = jnp.concatenate([v * keep0, v * keep1], axis=0)
        both = jnp.concatenate([both, diag], axis=1)
        o = jnp.dot(e, both, preferred_element_type=F32)
        outs.append((o[:, :128] / o[:, 128:]).astype(BF16))
    return outs


def natural_of_quad(shape, axis):
    n = lax.broadcasted_iota(jnp.int32, shape, axis)
    u, v, r, c = (n >> 5) & 1, (n >> 4) & 1, (n >> 2) & 3, n & 3
    return (u * 4 + r) * 8 + v * 4 + c


def kernel(
    field, w_qkv, w_proj, gains, pos_bias, out,
    x, wqkv, wproj, gain, bias, bias0, bias1, normed, qkv, ctx, ext, q1, kv1, ctxq,
    load_sem, out_sem, send_sem, recv_sem,
):
    lat, lon = lax.axis_index("lat"), lax.axis_index("lon")
    n_lat, n_lon = lax.axis_size("lat"), lax.axis_size("lon")

    def partner(dy, dx):
        there = {"lat": lax.rem(lat + dy + n_lat, n_lat), "lon": lax.rem(lon + dx + n_lon, n_lon)}
        return there

    barrier = pltpu.get_barrier_semaphore()
    for dy, dx in ROUTES:
        pl.semaphore_signal(barrier, inc=1, device_id=partner(dy, dx), device_id_type=MESH)

    loads = []

    def load(src, dst):
        copy = pltpu.make_async_copy(src, dst, load_sem.at[len(loads)])
        loads.append(copy)
        return copy

    ld_x = load(field, x)
    ld_gain = load(gains, gain)
    ld_qkv = [
        [load(w_qkv.at[s, :, pl.ds(D * c, D)], wqkv.at[s, :, pl.ds(D * c, D)]) for c in range(3)]
        for s in range(2)
    ]
    ld_bias = [load(pos_bias.at[s], bias.at[s]) for s in range(2)]
    ld_proj = [load(w_proj.at[s], wproj.at[s]) for s in range(2)]
    for copy in [ld_x, ld_gain, *ld_qkv[0], ld_bias[0], ld_proj[0]]:
        copy.start()

    ld_x.wait()
    ld_gain.wait()
    windows = [(i, j) for i in range(2) for j in range(2)]
    for w, (i, j) in enumerate(windows):
        cells = x[8 * i:8 * i + 8, 8 * j:8 * j + 8, :].reshape(WIN, D)
        normed[WIN * w:WIN * w + WIN, :] = layer_norm(cells, gain[0:1, :]).astype(BF16)
    for copy in [*ld_qkv[1], ld_bias[1], ld_proj[1]]:
        copy.start()
    for c in range(3):
        ld_qkv[0][c].wait()
        part = jnp.dot(normed[...], wqkv[0, :, D * c:D * c + D], preferred_element_type=F32)
        if c == 0:
            part = part * 0.125
        qkv[:, D * c:D * c + D] = part.astype(BF16)
    ld_bias[0].wait()
    for p in range(PAIRS):
        bias0[p] = jnp.concatenate([bias[0, 2 * p], bias[0, 2 * p + 1]], axis=1)
    for w in range(4):
        rows = slice(WIN * w, WIN * w + WIN)
        cols = [slice(128 * p, 128 * p + 128) for p in range(PAIRS)]
        outs = attend(
            [qkv[rows, 128 * p:128 * p + 128] for p in range(PAIRS)],
            [qkv[rows, D + 128 * p:D + 128 * p + 128] for p in range(PAIRS)],
            [qkv[rows, 2 * D + 128 * p:2 * D + 128 * p + 128] for p in range(PAIRS)],
            [bias0[p] for p in range(PAIRS)],
        )
        for p in range(PAIRS):
            ctx[rows, cols[p]] = outs[p]
    ld_proj[0].wait()
    update = jnp.dot(ctx[...], wproj[0], preferred_element_type=F32)

    quad_rows = (
        natural_of_quad((WIN, WIN), 0) == lax.broadcasted_iota(jnp.int32, (WIN, WIN), 1)
    ).astype(F32)
    nat_rows = (
        natural_of_quad((WIN, WIN), 1) == lax.broadcasted_iota(jnp.int32, (WIN, WIN), 0)
    ).astype(F32)
    for w, (i, j) in enumerate(windows):
        cells = x[8 * i:8 * i + 8, 8 * j:8 * j + 8, :].reshape(WIN, D)
        cells = cells + update[WIN * w:WIN * w + WIN, :]
        x[8 * i:8 * i + 8, 8 * j:8 * j + 8, :] = cells.reshape(8, 8, D)
        unit = layer_norm(cells, gain[1:2, :]).astype(BF16)
        unit = jnp.dot(quad_rows.astype(BF16), unit, preferred_element_type=F32).astype(BF16)
        ext[1 + 2 * i:3 + 2 * i, 1 + 2 * j:3 + 2 * j] = unit.reshape(2, 2, QUAD, D)

    pl.semaphore_wait(barrier, len(ROUTES))
    sends = []
    for n, (dy, dx) in enumerate(ROUTES):
        (src_r, dst_r), (src_c, dst_c) = route_slices(dy), route_slices(dx)
        copy = pltpu.make_async_remote_copy(
            src_ref=ext.at[src_r, src_c],
            dst_ref=ext.at[dst_r, dst_c],
            send_sem=send_sem.at[n],
            recv_sem=recv_sem.at[n],
            device_id=partner(dy, dx),
            device_id_type=MESH,
        )
        copy.start()
        sends.append(copy)

    for copy in ld_qkv[1]:
        copy.wait()
    own = ext[1:5, 1:5].reshape(256, D)
    own_q = jnp.dot(own, wqkv[1, :, :D], preferred_element_type=F32) * 0.125
    q1[...] = own_q.astype(BF16).reshape(4, 4, QUAD, D)
    own_kv = jnp.dot(own, wqkv[1, :, D:], preferred_element_type=F32)
    kv1[1:5, 1:5] = own_kv.astype(BF16).reshape(4, 4, QUAD, 2 * D)
    ld_bias[1].wait()
    twice = jnp.concatenate(
        [
            jnp.concatenate([nat_rows, jnp.zeros_like(nat_rows)], axis=1),
            jnp.concatenate([jnp.zeros_like(nat_rows), nat_rows], axis=1),
        ],
        axis=0,
    )
    for p in range(PAIRS):
        b = jnp.concatenate([bias[1, 2 * p], bias[1, 2 * p + 1]], axis=1)
        b = jnp.dot(quad_rows, b, precision=lax.Precision.HIGHEST, preferred_element_type=F32)
        b = jnp.dot(b, twice, precision=lax.Precision.HIGHEST, preferred_element_type=F32)
        bias1[p] = b.reshape(2, 2, QUAD, 128)

    lane = lax.broadcasted_iota(jnp.int32, (1, 128), 1)
    north = (lane & 63) < 32
    closed_n = jnp.where(lat == 0, -1e30, 0.0)
    closed_s = jnp.where(lat == n_lat - 1, -1e30, 0.0)

    def shifted(a, b):
        r0, r1 = max(2 * a - 1, 0), min(2 * a, 3) + 1
        c0, c1 = max(2 * b - 1, 0), min(2 * b, 3) + 1
        u0, v0 = r0 - (2 * a - 1), c0 - (2 * b - 1)
        nr, nc = r1 - r0, c1 - c0
        count = nr * nc * QUAD
        biases = []
        for p in range(PAIRS):
            part = bias1[p, u0:u0 + nr, v0:v0 + nc].reshape(count, 128)
            if a == 0:
                part = part + jnp.where(north, closed_n, 0.0)
            if a == 2:
                part = part + jnp.where(north, 0.0, closed_s)
            biases.append(part)
        here = (slice(2 * a, 2 * a + 2), slice(2 * b, 2 * b + 2), slice(None))
        outs = attend(
            [q1[r0:r1, c0:c1, :, 128 * p:128 * p + 128].reshape(count, 128) for p in range(PAIRS)],
            [kv1[(*here, slice(128 * p, 128 * p + 128))].reshape(WIN, 128) for p in range(PAIRS)],
            [kv1[(*here, slice(D + 128 * p, D + 128 * p + 128))].reshape(WIN, 128) for p in range(PAIRS)],
            biases,
        )
        for p in range(PAIRS):
            ctxq[r0:r1, c0:c1, :, 128 * p:128 * p + 128] = outs[p].reshape(nr, nc, QUAD, 128)

    shifted(1, 1)

    def halo_kv(units):
        return jnp.dot(units, wqkv[1, :, D:], preferred_element_type=F32).astype(BF16)

    sends[2].wait_recv()
    sends[3].wait_recv()
    units = jnp.concatenate([ext[1:5, 0].reshape(64, D), ext[1:5, 5].reshape(64, D)], axis=0)
    got = halo_kv(units)
    kv1[1:5, 0] = got[:64].reshape(4, QUAD, 2 * D)
    kv1[1:5, 5] = got[64:].reshape(4, QUAD, 2 * D)
    shifted(1, 0)
    shifted(1, 2)
    for n in (0, 1, 4, 5, 6, 7):
        sends[n].wait_recv()
    units = jnp.concatenate([ext[0].reshape(96, D), ext[5].reshape(96, D)], axis=0)
    got = halo_kv(units)
    kv1[0] = got[:96].reshape(6, QUAD, 2 * D)
    kv1[5] = got[96:].reshape(6, QUAD, 2 * D)
    for b in range(3):
        shifted(0, b)
        shifted(2, b)

    for w, (i, j) in enumerate(windows):
        block = ctxq[2 * i:2 * i + 2, 2 * j:2 * j + 2].reshape(WIN, D)
        block = jnp.dot(nat_rows.astype(BF16), block, preferred_element_type=F32)
        ctx[WIN * w:WIN * w + WIN, :] = block.astype(BF16)
    ld_proj[1].wait()
    update = jnp.dot(ctx[...], wproj[1], preferred_element_type=F32)
    for w, (i, j) in enumerate(windows):
        cells = x[8 * i:8 * i + 8, 8 * j:8 * j + 8, :].reshape(WIN, D)
        cells = cells + update[WIN * w:WIN * w + WIN, :]
        x[8 * i:8 * i + 8, 8 * j:8 * j + 8, :] = cells.reshape(8, 8, D)
    store = pltpu.make_async_copy(x, out, out_sem)
    store.start()
    for copy in sends:
        copy.wait_send()
    store.wait()


def on_device(field, w_qkv, w_proj, norm_gain, pos_bias):
    rows, cols, width = field.shape
    any_space = pl.BlockSpec(memory_space=pl.ANY)
    vmem = pltpu.VMEM
    return pl.pallas_call(
        kernel,
        out_shape=jax.ShapeDtypeStruct(field.shape, F32),
        in_specs=[any_space] * 5,
        out_specs=any_space,
        scratch_shapes=[
            vmem((rows, cols, D), F32),
            vmem((2, D, 3 * D), BF16),
            vmem((2, D, D), BF16),
            vmem((2, D), F32),
            vmem((2, HEADS, WIN, WIN), F32),
            vmem((PAIRS, WIN, 128), F32),
            vmem((PAIRS, 2, 2, QUAD, 128), F32),
            vmem((256, D), BF16),
            vmem((256, 3 * D), BF16),
            vmem((256, D), BF16),
            vmem((6, 6, QUAD, D), BF16),
            vmem((4, 4, QUAD, D), BF16),
            vmem((6, 6, QUAD, 2 * D), BF16),
            vmem((4, 4, QUAD, D), BF16),
            pltpu.SemaphoreType.DMA((12,)),
            pltpu.SemaphoreType.DMA,
            pltpu.SemaphoreType.DMA((len(ROUTES),)),
            pltpu.SemaphoreType.DMA((len(ROUTES),)),
        ],
        compiler_params=pltpu.CompilerParams(
            collective_id=0, has_side_effects=True, vmem_limit_bytes=48 * 1024 * 1024
        ),
        cost_estimate=pl.CostEstimate(
            flops=3_300_000_000, bytes_accessed=13_000_000, transcendentals=400_000
        ),
        name="swin_pair",
    )(field, w_qkv, w_proj, norm_gain, pos_bias)


def solution(mesh):
    return jax.shard_map(
        on_device,
        mesh=mesh,
        in_specs=(P("lat", "lon", None), P(), P(), P(), P()),
        out_specs=P("lat", "lon", None),
        check_vma=False,
    )
```

```python
import functools

import jax
import jax.numpy as jnp
from jax import lax
from jax.experimental import pallas as pl
from jax.experimental.pallas import tpu as pltpu
from jax.sharding import PartitionSpec as P

D = 768
HEADS = 12
PAIRS = HEADS // 2
WIN = 64
QUAD = 16
F32 = jnp.float32
BF16 = jnp.bfloat16
MESH = pl.DeviceIdType.MESH
NT = (((1,), (1,)), ((), ()))

PEERS = ((-1, 0), (1, 0), (0, -1), (0, 1), (-1, -1), (-1, 1), (1, -1), (1, 1))
OWN = slice(1, 5)


def piece(dy, dx, rows=OWN):
    def axis(step, run):
        if step == 0:
            return pl.ds(run.start, run.stop - run.start), pl.ds(run.start, run.stop - run.start)
        return (pl.ds(1, 1), pl.ds(5, 1)) if step < 0 else (pl.ds(4, 1), pl.ds(0, 1))

    (src_r, dst_r), (src_c, dst_c) = axis(dy, rows), axis(dx, OWN)
    return dy, dx, (src_r, src_c), (dst_r, dst_c)


WAVES = tuple(
    (
        piece(dy, 0), piece(dy, -1), piece(dy, 1),
        piece(0, -1, slice(top, top + 2)), piece(0, 1, slice(top, top + 2)),
    )
    for dy, top in ((-1, 1), (1, 3))
)


def layer_norm(x, gain):
    mean = jnp.mean(x, axis=-1, keepdims=True)
    centred = x - mean
    var = jnp.mean(centred * centred, axis=-1, keepdims=True)
    return centred * lax.rsqrt(var + 1e-05) * gain


def lanes_low(shape, axis):
    return lax.broadcasted_iota(jnp.int32, shape, axis) < 64


def attend(qs, ks, vs, biases):
    low = lanes_low((1, 128), 1)
    keep0 = low.astype(F32).astype(BF16)
    keep1 = (1.0 - low.astype(F32)).astype(BF16)
    diag = (lanes_low((128, 128), 0) == lanes_low((128, 128), 1)).astype(F32).astype(BF16)
    scores = []
    for q, k, bias in zip(qs, ks, biases):
        both = jnp.concatenate([k * keep0, k * keep1], axis=0)
        scores.append(lax.dot_general(q, both, NT, preferred_element_type=F32) + bias)
    tops = []
    for s in scores:
        top0 = jnp.max(jnp.where(low, s, -jnp.inf), axis=-1, keepdims=True)
        top1 = jnp.max(jnp.where(low, -jnp.inf, s), axis=-1, keepdims=True)
        tops.append(jnp.where(low, top0, top1))
    expos = [jnp.exp(s - top).astype(BF16) for s, top in zip(scores, tops)]
    outs = []
    for e, v in zip(expos, vs):
        both = jnp.concatenate([v * keep0, v * keep1], axis=0)
        both = jnp.concatenate([both, diag], axis=1)
        o = jnp.dot(e, both, preferred_element_type=F32)
        outs.append((o[:, :128] / o[:, 128:]).astype(BF16))
    return outs


def halves(width):
    return lax.broadcasted_iota(jnp.int32, (1, 8, width), 1) < 4


def to_quads(cells):
    n, _, width = cells.shape
    pairs = cells.reshape(n // 2, 2, 8, width)
    even, odd = pairs[:, 0], pairs[:, 1]
    left = jnp.where(halves(width), even, pltpu.roll(odd, 4, 1))
    right = jnp.where(halves(width), pltpu.roll(even, 4, 1), odd)
    return left, right


def from_quads(left, right):
    n, _, width = left.shape
    even = jnp.where(halves(width), left, pltpu.roll(right, 4, 1))
    odd = jnp.where(halves(width), pltpu.roll(left, 4, 1), right)
    return jnp.stack([even, odd], axis=1).reshape(2 * n, 8, width)


def window_quads(cells):
    width = cells.shape[-1]
    left, right = to_quads(cells)
    both = [side.reshape(2, QUAD, width) for side in (left, right)]
    return jnp.stack(both, axis=1)


def natural_of_quad(shape, axis):
    n = lax.broadcasted_iota(jnp.int32, shape, axis)
    u, v, r, c = (n >> 5) & 1, (n >> 4) & 1, (n >> 2) & 3, n & 3
    return (u * 4 + r) * 8 + v * 4 + c


def kernel(
    field, w_qkv, w_proj, gains, pos_bias, out,
    x, xq, wqkv, wproj, gain, bias, bias0, bias1, normed, nquad, q0, kv0, ext, q1, kv1, ctx,
    load_sem, out_sem, send_sem, recv_sem,
):
    lat, lon = lax.axis_index("lat"), lax.axis_index("lon")
    n_lat, n_lon = lax.axis_size("lat"), lax.axis_size("lon")

    def partner(dy, dx):
        return {"lat": lax.rem(lat + dy + n_lat, n_lat), "lon": lax.rem(lon + dx + n_lon, n_lon)}

    def where_inside(dy, act):
        if dy == 0:
            act()
        else:
            pl.when(lat > 0 if dy < 0 else lat < n_lat - 1)(act)

    barrier = pltpu.get_barrier_semaphore()
    for dy, dx in PEERS:
        where_inside(dy, lambda: pl.semaphore_signal(
            barrier, inc=1, device_id=partner(dy, dx), device_id_type=MESH))

    loads = []

    def load(src, dst):
        copy = pltpu.make_async_copy(src, dst, load_sem.at[len(loads)])
        loads.append(copy)
        return copy

    ld_x = load(field, x)
    ld_gain = load(gains, gain)
    ld_qkv = [
        [load(w_qkv.at[s, :, pl.ds(D * c, D)], wqkv.at[s, :, pl.ds(D * c, D)]) for c in range(3)]
        for s in range(2)
    ]
    ld_bias = [load(pos_bias.at[s], bias.at[s]) for s in range(2)]
    ld_proj = [load(w_proj.at[s], wproj.at[s]) for s in range(2)]
    for copy in [ld_x, ld_gain, *ld_qkv[0], ld_bias[0], ld_proj[0]]:
        copy.start()

    ld_x.wait()
    ld_gain.wait()
    for i in range(2):
        for j in range(2):
            w = 2 * i + j
            quads = (slice(2 * i, 2 * i + 2), slice(2 * j, 2 * j + 2))
            cells = x[8 * i:8 * i + 8, 8 * j:8 * j + 8, :]
            unit = layer_norm(cells, gain[0:1, :])
            normed[WIN * w:WIN * w + WIN, :] = unit.reshape(WIN, D).astype(BF16)
            nquad[quads] = window_quads(unit).astype(BF16)
            xq[quads] = window_quads(cells)
    ld_qkv[0][0].wait()
    part = jnp.dot(nquad[...].reshape(256, D), wqkv[0, :, :D], preferred_element_type=F32) * 0.125
    q0[...] = part.astype(BF16).reshape(4, 4, QUAD, D)
    for c in range(2):
        ld_qkv[0][1 + c].wait()
        part = jnp.dot(
            normed[...], wqkv[0, :, D + D * c:2 * D + D * c], preferred_element_type=F32
        )
        kv0[:, D * c:D * c + D] = part.astype(BF16)
    ld_bias[0].wait()

    def pair_bias(s, p):
        b = jnp.concatenate([bias[s, 2 * p], bias[s, 2 * p + 1]], axis=1)
        return window_quads(b.reshape(8, 8, 128)).reshape(WIN, 128)

    for p in range(PAIRS):
        bias0[p] = pair_bias(0, p)
    ld_proj[0].wait()
    for copy in [*ld_qkv[1], ld_bias[1], ld_proj[1]]:
        copy.start()

    sends = []

    def send(n, dy, dx, src, dst):
        copy = pltpu.make_async_remote_copy(
            src_ref=ext.at[src],
            dst_ref=ext.at[dst],
            send_sem=send_sem.at[n],
            recv_sem=recv_sem.at[n],
            device_id=partner(dy, dx),
            device_id_type=MESH,
        )
        sends.append((dy, dx, copy))
        where_inside(dy, copy.start)

    def arrived(dy, dx):
        for route_y, route_x, copy in sends:
            if (route_y, route_x) == (dy, dx):
                where_inside(-dy, copy.wait_recv)

    for i in range(2):
        jobs = [(j, p) for j in range(2) for p in range(PAIRS)]
        quads = [(slice(2 * i, 2 * i + 2), slice(2 * j, 2 * j + 2), slice(None)) for j in range(2)]
        rows = [slice(WIN * (2 * i + j), WIN * (2 * i + j) + WIN) for j in range(2)]
        cols = [slice(128 * p, 128 * p + 128) for p in range(PAIRS)]
        outs = attend(
            [q0[(*quads[j], cols[p])].reshape(WIN, 128) for j, p in jobs],
            [kv0[rows[j], cols[p]] for j, p in jobs],
            [kv0[rows[j], D + 128 * p:D + 128 * p + 128] for j, p in jobs],
            [bias0[p] for j, p in jobs],
        )
        for (j, p), o in zip(jobs, outs):
            ctx[(*quads[j], cols[p])] = o.reshape(2, 2, QUAD, 128)
        band = slice(2 * i, 2 * i + 2)
        update = jnp.dot(ctx[band].reshape(128, D), wproj[0], preferred_element_type=F32)
        cells = xq[band].reshape(128, D) + update
        xq[band] = cells.reshape(2, 4, QUAD, D)
        unit = layer_norm(cells, gain[1:2, :]).astype(BF16)
        ext[1 + 2 * i:3 + 2 * i, OWN] = unit.reshape(2, 4, QUAD, D)
        if i == 0:
            inner = (lat > 0) & (lat < n_lat - 1)
            pl.when(inner)(lambda: pl.semaphore_wait(barrier, 8))
            pl.when(jnp.logical_not(inner))(lambda: pl.semaphore_wait(barrier, 5))
        for n, route in enumerate(WAVES[i]):
            send(len(WAVES[0]) * i + n, *route)

    for copy in ld_qkv[1]:
        copy.wait()
    own = ext[OWN, OWN].reshape(256, D)
    own_q = jnp.dot(own, wqkv[1, :, :D], preferred_element_type=F32) * 0.125
    q1[...] = own_q.astype(BF16).reshape(4, 4, QUAD, D)
    own_kv = jnp.dot(own, wqkv[1, :, D:], preferred_element_type=F32)
    kv1[OWN, OWN] = own_kv.astype(BF16).reshape(4, 4, QUAD, 2 * D)
    ld_bias[1].wait()
    ld_proj[1].wait()
    row = lax.broadcasted_iota(jnp.int32, (128, 128), 0)
    lane = lax.broadcasted_iota(jnp.int32, (128, 128), 1)
    key_order = (natural_of_quad((128, 128), 1) + (lane & 64) == row).astype(F32)
    for p in range(PAIRS):
        b = jnp.dot(
            pair_bias(1, p), key_order, precision=lax.Precision.HIGHEST, preferred_element_type=F32
        )
        bias1[p] = b.reshape(2, 2, QUAD, 128)

    @pl.when(lat == 0)
    def _():
        ext[0] = jnp.zeros((6, QUAD, D), BF16)

    @pl.when(lat == n_lat - 1)
    def _():
        ext[5] = jnp.zeros((6, QUAD, D), BF16)

    north = (lax.broadcasted_iota(jnp.int32, (1, 128), 1) & 63) < 32
    closed = {
        0: jnp.where(north, jnp.where(lat == 0, -1e30, 0.0), 0.0),
        2: jnp.where(north, 0.0, jnp.where(lat == n_lat - 1, -1e30, 0.0)),
    }

    def shifted(group):
        qs, ks, vs, biases, places = [], [], [], [], []
        for a, b in group:
            r0, r1 = max(2 * a - 1, 0), min(2 * a, 3) + 1
            c0, c1 = max(2 * b - 1, 0), min(2 * b, 3) + 1
            u0, v0 = r0 - (2 * a - 1), c0 - (2 * b - 1)
            nr, nc = r1 - r0, c1 - c0
            count = nr * nc * QUAD
            here = (slice(2 * a, 2 * a + 2), slice(2 * b, 2 * b + 2), slice(None))
            for p in range(PAIRS):
                col = slice(128 * p, 128 * p + 128)
                place = (slice(r0, r1), slice(c0, c1), slice(None), col)
                part = bias1[p, u0:u0 + nr, v0:v0 + nc].reshape(count, 128)
                if a in closed:
                    part = part + closed[a]
                biases.append(part)
                qs.append(q1[place].reshape(count, 128))
                ks.append(kv1[(*here, col)].reshape(WIN, 128))
                vs.append(kv1[(*here, slice(D + 128 * p, D + 128 * p + 128))].reshape(WIN, 128))
                places.append((place, (nr, nc, QUAD, 128)))
        for (place, shape), o in zip(places, attend(qs, ks, vs, biases)):
            ctx[place] = o.reshape(shape)

    def halo_kv(units):
        return jnp.dot(units, wqkv[1, :, D:], preferred_element_type=F32).astype(BF16)

    stores = []

    def finish(bands):
        block = jnp.concatenate([ctx[r].reshape(WIN, D) for r in bands], axis=0)
        update = jnp.dot(block, wproj[1], preferred_element_type=F32)
        for n, r in enumerate(bands):
            cells = xq[r] + update[WIN * n:WIN * n + WIN].reshape(4, QUAD, D)
            for j in range(2):
                left, right = [cells[2 * j + v].reshape(2, 8, D) for v in range(2)]
                x[4 * r:4 * r + 4, 8 * j:8 * j + 8, :] = from_quads(left, right)
            rows = pl.ds(4 * r, 4)
            store = pltpu.make_async_copy(x.at[rows], out.at[rows], out_sem.at[r])
            store.start()
            stores.append(store)

    shifted([(1, 1)])
    arrived(0, -1)
    arrived(0, 1)
    units = jnp.concatenate([ext[OWN, 0].reshape(64, D), ext[OWN, 5].reshape(64, D)], axis=0)
    got = halo_kv(units)
    kv1[OWN, 0] = got[:64].reshape(4, QUAD, 2 * D)
    kv1[OWN, 5] = got[64:].reshape(4, QUAD, 2 * D)
    shifted([(1, 0), (1, 2)])
    finish([1, 2])
    for a, dy in ((2, -1), (0, 1)):
        for dx in (0, -1, 1):
            arrived(dy, dx)
        edge = 5 if a == 2 else 0
        kv1[edge] = halo_kv(ext[edge].reshape(96, D)).reshape(6, QUAD, 2 * D)
        shifted([(a, 0), (a, 1), (a, 2)])
    finish([0, 3])
    for dy, _, copy in sends:
        where_inside(dy, copy.wait_send)
    for store in stores:
        store.wait()


def on_device(field, w_qkv, w_proj, norm_gain, pos_bias):
    rows, cols, width = field.shape
    any_space = pl.BlockSpec(memory_space=pl.ANY)
    vmem = pltpu.VMEM
    return pl.pallas_call(
        kernel,
        out_shape=jax.ShapeDtypeStruct(field.shape, F32),
        in_specs=[any_space] * 5,
        out_specs=any_space,
        scratch_shapes=[
            vmem((rows, cols, D), F32),
            vmem((4, 4, QUAD, D), F32),
            vmem((2, D, 3 * D), BF16),
            vmem((2, D, D), BF16),
            vmem((2, D), F32),
            vmem((2, HEADS, WIN, WIN), F32),
            vmem((PAIRS, WIN, 128), F32),
            vmem((PAIRS, 2, 2, QUAD, 128), F32),
            vmem((256, D), BF16),
            vmem((4, 4, QUAD, D), BF16),
            vmem((4, 4, QUAD, D), BF16),
            vmem((256, 2 * D), BF16),
            vmem((6, 6, QUAD, D), BF16),
            vmem((4, 4, QUAD, D), BF16),
            vmem((6, 6, QUAD, 2 * D), BF16),
            vmem((4, 4, QUAD, D), BF16),
            pltpu.SemaphoreType.DMA((12,)),
            pltpu.SemaphoreType.DMA((4,)),
            pltpu.SemaphoreType.DMA((10,)),
            pltpu.SemaphoreType.DMA((10,)),
        ],
        compiler_params=pltpu.CompilerParams(
            collective_id=0, has_side_effects=True, vmem_limit_bytes=48 * 1024 * 1024
        ),
        cost_estimate=pl.CostEstimate(
            flops=3_300_000_000, bytes_accessed=13_000_000, transcendentals=400_000
        ),
        name="swin_pair",
    )(*[pltpu.with_memory_space_constraint(a, pltpu.HBM) for a in (field, w_qkv, w_proj, norm_gain, pos_bias)])


def solution(mesh):
    return jax.shard_map(
        on_device,
        mesh=mesh,
        in_specs=(P("lat", "lon", None), P(), P(), P(), P()),
        out_specs=P("lat", "lon", None),
        check_vma=False,
    )
```

```python
import functools

import jax
import jax.numpy as jnp
from jax import lax
from jax.experimental import pallas as pl
from jax.experimental.pallas import tpu as pltpu
from jax.sharding import PartitionSpec as P

D = 768
HEADS = 12
PAIRS = HEADS // 2
WIN = 64
QUAD = 16
F32 = jnp.float32
BF16 = jnp.bfloat16
MESH = pl.DeviceIdType.MESH
NT = (((1,), (1,)), ((), ()))

PEERS = ((-1, 0), (1, 0), (0, -1), (0, 1), (-1, -1), (-1, 1), (1, -1), (1, 1))
OWN = slice(1, 5)
WAVE = 5


def layer_norm(x, gain):
    mean = jnp.mean(x, axis=-1, keepdims=True)
    centred = x - mean
    var = jnp.mean(centred * centred, axis=-1, keepdims=True)
    return centred * lax.rsqrt(var + 1e-05) * gain


def lanes_low(shape, axis):
    return lax.broadcasted_iota(jnp.int32, shape, axis) < 64


def attend(qs, ks, vs, biases):
    low = lanes_low((1, 128), 1)
    keep0 = low.astype(F32).astype(BF16)
    keep1 = (1.0 - low.astype(F32)).astype(BF16)
    diag = (lanes_low((128, 128), 0) == lanes_low((128, 128), 1)).astype(F32).astype(BF16)
    scores = []
    for q, k, bias in zip(qs, ks, biases):
        both = jnp.concatenate([k * keep0, k * keep1], axis=0)
        scores.append(lax.dot_general(q, both, NT, preferred_element_type=F32) + bias)
    tops = []
    for s in scores:
        top0 = jnp.max(jnp.where(low, s, -jnp.inf), axis=-1, keepdims=True)
        top1 = jnp.max(jnp.where(low, -jnp.inf, s), axis=-1, keepdims=True)
        tops.append(jnp.where(low, top0, top1))
    expos = [jnp.exp(s - top).astype(BF16) for s, top in zip(scores, tops)]
    outs = []
    for e, v in zip(expos, vs):
        both = jnp.concatenate([v * keep0, v * keep1], axis=0)
        both = jnp.concatenate([both, diag], axis=1)
        o = jnp.dot(e, both, preferred_element_type=F32)
        outs.append((o[:, :128] / o[:, 128:]).astype(BF16))
    return outs


def halves(width):
    return lax.broadcasted_iota(jnp.int32, (1, 8, width), 1) < 4


def to_quads(cells):
    n, _, width = cells.shape
    pairs = cells.reshape(n // 2, 2, 8, width)
    even, odd = pairs[:, 0], pairs[:, 1]
    left = jnp.where(halves(width), even, pltpu.roll(odd, 4, 1))
    right = jnp.where(halves(width), pltpu.roll(even, 4, 1), odd)
    return left, right


def from_quads(left, right):
    n, _, width = left.shape
    even = jnp.where(halves(width), left, pltpu.roll(right, 4, 1))
    odd = jnp.where(halves(width), pltpu.roll(left, 4, 1), right)
    return jnp.stack([even, odd], axis=1).reshape(2 * n, 8, width)


def window_quads(cells):
    width = cells.shape[-1]
    left, right = to_quads(cells)
    both = [side.reshape(2, QUAD, width) for side in (left, right)]
    return jnp.stack(both, axis=1)


def natural_of_quad(shape, axis):
    n = lax.broadcasted_iota(jnp.int32, shape, axis)
    u, v, r, c = (n >> 5) & 1, (n >> 4) & 1, (n >> 2) & 3, n & 3
    return (u * 4 + r) * 8 + v * 4 + c


def kernel(
    field, w_qkv, w_proj, gains, pos_bias, out,
    x, xq, wqkv, wproj, gain, bias, bias0, bias1, normed, nquad, q0, kv0, ext, q1, kv1, ctx,
    load_sem, out_sem, send_sem, recv_sem,
):
    lat, lon = lax.axis_index("lat"), lax.axis_index("lon")
    n_lat, n_lon = lax.axis_size("lat"), lax.axis_size("lon")

    def partner(dy, dx):
        return {"lat": lax.rem(lat + dy + n_lat, n_lat), "lon": lax.rem(lon + dx + n_lon, n_lon)}

    def inside(dy):
        return (lat + dy >= 0) & (lat + dy < n_lat)

    odd = lax.rem(lat, 2)
    order = (odd, 1 - odd)

    barrier = pltpu.get_barrier_semaphore()
    for dy, dx in PEERS:
        pl.when(inside(dy))(lambda: pl.semaphore_signal(
            barrier, inc=1, device_id=partner(dy, dx), device_id_type=MESH))

    loads = []

    def load(src, dst):
        copy = pltpu.make_async_copy(src, dst, load_sem.at[len(loads)])
        loads.append(copy)
        return copy

    ld_x = load(field, x)
    ld_gain = load(gains, gain)
    ld_qkv = [
        [load(w_qkv.at[s, :, pl.ds(D * c, D)], wqkv.at[s, :, pl.ds(D * c, D)]) for c in range(3)]
        for s in range(2)
    ]
    ld_bias = [load(pos_bias.at[s], bias.at[s]) for s in range(2)]
    ld_proj = [load(w_proj.at[s], wproj.at[s]) for s in range(2)]
    for copy in [ld_x, ld_gain, *ld_qkv[0], ld_bias[0], ld_proj[0]]:
        copy.start()

    ld_x.wait()
    ld_gain.wait()
    for i in range(2):
        for j in range(2):
            w = 2 * i + j
            quads = (slice(2 * i, 2 * i + 2), slice(2 * j, 2 * j + 2))
            cells = x[8 * i:8 * i + 8, 8 * j:8 * j + 8, :]
            unit = layer_norm(cells, gain[0:1, :])
            normed[WIN * w:WIN * w + WIN, :] = unit.reshape(WIN, D).astype(BF16)
            nquad[quads] = window_quads(unit).astype(BF16)
            xq[quads] = window_quads(cells)
    ld_qkv[0][0].wait()
    part = jnp.dot(nquad[...].reshape(256, D), wqkv[0, :, :D], preferred_element_type=F32) * 0.125
    q0[...] = part.astype(BF16).reshape(4, 4, QUAD, D)
    for c in range(2):
        ld_qkv[0][1 + c].wait()
        part = jnp.dot(
            normed[...], wqkv[0, :, D + D * c:2 * D + D * c], preferred_element_type=F32
        )
        kv0[:, :, D * c:D * c + D] = part.astype(BF16).reshape(4, WIN, D)
    ld_bias[0].wait()

    def pair_bias(s, p):
        b = jnp.concatenate([bias[s, 2 * p], bias[s, 2 * p + 1]], axis=1)
        return window_quads(b.reshape(8, 8, 128)).reshape(WIN, 128)

    for p in range(PAIRS):
        bias0[p] = pair_bias(0, p)

    waves = ([], [])

    def send(wave, dy, dx, src, dst):
        n = WAVE * wave + len(waves[wave])
        copy = pltpu.make_async_remote_copy(
            src_ref=ext.at[src],
            dst_ref=ext.at[dst],
            send_sem=send_sem.at[n],
            recv_sem=recv_sem.at[n],
            device_id=partner(dy, dx),
            device_id_type=MESH,
        )
        waves[wave].append(copy)
        return copy

    for wave, i in enumerate(order):
        band = pl.ds(2 * i, 2)
        jobs = [(j, p) for j in range(2) for p in range(PAIRS)]
        quads = [(band, slice(2 * j, 2 * j + 2), slice(None)) for j in range(2)]
        cols = [slice(128 * p, 128 * p + 128) for p in range(PAIRS)]
        outs = attend(
            [q0[(*quads[j], cols[p])].reshape(WIN, 128) for j, p in jobs],
            [kv0[pl.ds(2 * i + j, 1), :, cols[p]].reshape(WIN, 128) for j, p in jobs],
            [kv0[pl.ds(2 * i + j, 1), :, D + 128 * p:D + 128 * p + 128].reshape(WIN, 128) for j, p in jobs],
            [bias0[p] for j, p in jobs],
        )
        for (j, p), o in zip(jobs, outs):
            ctx[(*quads[j], cols[p])] = o.reshape(2, 2, QUAD, 128)
        if wave == 0:
            ld_proj[0].wait()
            for copy in [*ld_qkv[1], ld_bias[1], ld_proj[1]]:
                copy.start()
        update = jnp.dot(ctx[band].reshape(128, D), wproj[0], preferred_element_type=F32)
        cells = xq[band].reshape(128, D) + update
        xq[band] = cells.reshape(2, 4, QUAD, D)
        unit = layer_norm(cells, gain[1:2, :]).astype(BF16)
        ext[pl.ds(1 + 2 * i, 2), OWN] = unit.reshape(2, 4, QUAD, D)
        if wave == 0:
            inner = (lat > 0) & (lat < n_lat - 1)
            pl.when(inner)(lambda: pl.semaphore_wait(barrier, 8))
            pl.when(jnp.logical_not(inner))(lambda: pl.semaphore_wait(barrier, 5))
        half = pl.ds(1 + 2 * i, 2)
        send(wave, 0, -1, (half, slice(1, 2)), (half, slice(5, 6))).start()
        send(wave, 0, 1, (half, slice(4, 5)), (half, slice(0, 1))).start()
        dy = 2 * i - 1
        here, there = pl.ds(1 + 3 * i, 1), pl.ds(5 - 5 * i, 1)
        outward = (
            send(wave, dy, 0, (here, slice(1, 5)), (there, slice(1, 5))),
            send(wave, dy, -1, (here, slice(1, 2)), (there, slice(5, 6))),
            send(wave, dy, 1, (here, slice(4, 5)), (there, slice(0, 1))),
        )

        @pl.when(inside(dy))
        def _():
            for copy in outward:
                copy.start()

    for copy in ld_qkv[1]:
        copy.wait()
    own = ext[OWN, OWN].reshape(256, D)
    own_q = jnp.dot(own, wqkv[1, :, :D], preferred_element_type=F32) * 0.125
    q1[...] = own_q.astype(BF16).reshape(4, 4, QUAD, D)
    own_kv = jnp.dot(own, wqkv[1, :, D:], preferred_element_type=F32)
    kv1[OWN, OWN] = own_kv.astype(BF16).reshape(4, 4, QUAD, 2 * D)
    ld_bias[1].wait()
    ld_proj[1].wait()
    row = lax.broadcasted_iota(jnp.int32, (128, 128), 0)
    lane = lax.broadcasted_iota(jnp.int32, (128, 128), 1)
    key_order = (natural_of_quad((128, 128), 1) + (lane & 64) == row).astype(F32)
    for p in range(PAIRS):
        b = jnp.dot(
            pair_bias(1, p), key_order, precision=lax.Precision.HIGHEST, preferred_element_type=F32
        )
        bias1[p] = b.reshape(2, 2, QUAD, 128)

    @pl.when(lat == 0)
    def _():
        ext[0] = jnp.zeros((6, QUAD, D), BF16)

    @pl.when(lat == n_lat - 1)
    def _():
        ext[5] = jnp.zeros((6, QUAD, D), BF16)

    north = (lax.broadcasted_iota(jnp.int32, (1, 128), 1) & 63) < 32

    def shifted(group):
        qs, ks, vs, biases, places = [], [], [], [], []
        for r0, nr, u0, k0, b, closed in group:
            c0, c1 = max(2 * b - 1, 0), min(2 * b, 3) + 1
            v0, nc = c0 - (2 * b - 1), c1 - c0
            count = nr * nc * QUAD
            here = (pl.ds(k0, 2), slice(2 * b, 2 * b + 2), slice(None))
            for p in range(PAIRS):
                col = slice(128 * p, 128 * p + 128)
                place = (pl.ds(r0, nr), slice(c0, c1), slice(None), col)
                part = bias1[p:p + 1, pl.ds(u0, nr), v0:v0 + nc].reshape(count, 128)
                biases.append(part if closed is None else part + closed)
                qs.append(q1[place].reshape(count, 128))
                ks.append(kv1[(*here, col)].reshape(WIN, 128))
                vs.append(kv1[(*here, slice(D + 128 * p, D + 128 * p + 128))].reshape(WIN, 128))
                places.append((place, (nr, nc, QUAD, 128)))
        for (place, shape), o in zip(places, attend(qs, ks, vs, biases)):
            ctx[place] = o.reshape(shape)

    middle = [(1, 2, 0, 2, b, None) for b in range(3)]

    def edge(i):
        shut = jnp.where(inside(2 * i - 1), 0.0, -1e30)
        closed = jnp.where(north, jnp.where(i == 0, shut, 0.0), jnp.where(i == 1, shut, 0.0))
        return [(3 * i, 1, 1 - i, 4 * i, b, closed) for b in range(3)]

    def halo_kv(units):
        return jnp.dot(units, wqkv[1, :, D:], preferred_element_type=F32).astype(BF16)

    stores = []

    def finish(bands):
        block = jnp.concatenate([ctx[r].reshape(WIN, D) for r in bands], axis=0)
        update = jnp.dot(block, wproj[1], preferred_element_type=F32)
        for n, r in enumerate(bands):
            cells = xq[r] + update[WIN * n:WIN * n + WIN].reshape(4, QUAD, D)
            for j in range(2):
                left, right = [cells[2 * j + v].reshape(2, 8, D) for v in range(2)]
                x[4 * r:4 * r + 4, 8 * j:8 * j + 8, :] = from_quads(left, right)
            rows = pl.ds(4 * r, 4)
            store = pltpu.make_async_copy(x.at[rows], out.at[rows], out_sem.at[r])
            store.start()
            stores.append(store)

    shifted([middle[1]])
    for wave in range(2):
        for copy in waves[wave][:2]:
            copy.wait_recv()

    def edge_arrived(wave):
        @pl.when(inside(2 * order[wave] - 1))
        def _():
            for copy in waves[wave][2:]:
                copy.wait_recv()

    edge_arrived(0)
    far = 5 * order[0]
    units = jnp.concatenate(
        [ext[OWN, 0].reshape(64, D), ext[OWN, 5].reshape(64, D), ext[far].reshape(96, D)], axis=0
    )
    got = halo_kv(units)
    kv1[OWN, 0] = got[:64].reshape(4, QUAD, 2 * D)
    kv1[OWN, 5] = got[64:128].reshape(4, QUAD, 2 * D)
    kv1[far] = got[128:].reshape(6, QUAD, 2 * D)
    shifted([middle[0], middle[2], *edge(order[0])])
    finish([1, 2])
    edge_arrived(1)
    far = 5 * order[1]
    kv1[far] = halo_kv(ext[far].reshape(96, D)).reshape(6, QUAD, 2 * D)
    shifted(edge(order[1]))
    finish([0, 3])
    for wave in range(2):
        for copy in waves[wave][:2]:
            copy.wait_send()

        @pl.when(inside(2 * order[wave] - 1))
        def _():
            for copy in waves[wave][2:]:
                copy.wait_send()

    for store in stores:
        store.wait()


def on_device(field, w_qkv, w_proj, norm_gain, pos_bias):
    rows, cols, width = field.shape
    any_space = pl.BlockSpec(memory_space=pl.ANY)
    vmem = pltpu.VMEM
    return pl.pallas_call(
        kernel,
        out_shape=jax.ShapeDtypeStruct(field.shape, F32),
        in_specs=[any_space] * 5,
        out_specs=any_space,
        scratch_shapes=[
            vmem((rows, cols, D), F32),
            vmem((4, 4, QUAD, D), F32),
            vmem((2, D, 3 * D), BF16),
            vmem((2, D, D), BF16),
            vmem((2, D), F32),
            vmem((2, HEADS, WIN, WIN), F32),
            vmem((PAIRS, WIN, 128), F32),
            vmem((PAIRS, 2, 2, QUAD, 128), F32),
            vmem((256, D), BF16),
            vmem((4, 4, QUAD, D), BF16),
            vmem((4, 4, QUAD, D), BF16),
            vmem((4, WIN, 2 * D), BF16),
            vmem((6, 6, QUAD, D), BF16),
            vmem((4, 4, QUAD, D), BF16),
            vmem((6, 6, QUAD, 2 * D), BF16),
            vmem((4, 4, QUAD, D), BF16),
            pltpu.SemaphoreType.DMA((12,)),
            pltpu.SemaphoreType.DMA((4,)),
            pltpu.SemaphoreType.DMA((2 * WAVE,)),
            pltpu.SemaphoreType.DMA((2 * WAVE,)),
        ],
        compiler_params=pltpu.CompilerParams(
            collective_id=0, has_side_effects=True, vmem_limit_bytes=48 * 1024 * 1024
        ),
        cost_estimate=pl.CostEstimate(
            flops=3_300_000_000, bytes_accessed=13_000_000, transcendentals=400_000
        ),
        name="swin_pair",
    )(*[pltpu.with_memory_space_constraint(a, pltpu.HBM) for a in (field, w_qkv, w_proj, norm_gain, pos_bias)])


def solution(mesh):
    return jax.shard_map(
        on_device,
        mesh=mesh,
        in_specs=(P("lat", "lon", None), P(), P(), P(), P()),
        out_specs=P("lat", "lon", None),
        check_vma=False,
    )
```

```python
import functools

import jax
import jax.numpy as jnp
from jax import lax
from jax.experimental import pallas as pl
from jax.experimental.pallas import tpu as pltpu
from jax.sharding import PartitionSpec as P

D = 768
HEADS = 12
PAIRS = HEADS // 2
WIN = 64
QUAD = 16
F32 = jnp.float32
BF16 = jnp.bfloat16
MESH = pl.DeviceIdType.MESH
NT = (((1,), (1,)), ((), ()))

PEERS = ((-1, 0), (1, 0), (0, -1), (0, 1), (-1, -1), (-1, 1), (1, -1), (1, 1))
OWN = slice(1, 5)
WAVE = 5


def layer_norm(x, gain):
    mean = jnp.mean(x, axis=-1, keepdims=True)
    centred = x - mean
    var = jnp.mean(centred * centred, axis=-1, keepdims=True)
    return centred * lax.rsqrt(var + 1e-05) * gain


def lanes_low(shape, axis):
    return lax.broadcasted_iota(jnp.int32, shape, axis) < 64


def attend(qs, ks, vs, biases):
    low = lanes_low((1, 128), 1)
    keep0 = low.astype(F32).astype(BF16)
    keep1 = (1.0 - low.astype(F32)).astype(BF16)
    diag = (lanes_low((128, 128), 0) == lanes_low((128, 128), 1)).astype(F32).astype(BF16)
    scores = []
    for q, k, bias in zip(qs, ks, biases):
        both = jnp.concatenate([k * keep0, k * keep1], axis=0)
        scores.append(lax.dot_general(q, both, NT, preferred_element_type=F32) + bias)
    tops = []
    for s in scores:
        top0 = jnp.max(jnp.where(low, s, -jnp.inf), axis=-1, keepdims=True)
        top1 = jnp.max(jnp.where(low, -jnp.inf, s), axis=-1, keepdims=True)
        tops.append(jnp.where(low, top0, top1))
    expos = [jnp.exp(s - top).astype(BF16) for s, top in zip(scores, tops)]
    outs = []
    for e, v in zip(expos, vs):
        both = jnp.concatenate([v * keep0, v * keep1], axis=0)
        both = jnp.concatenate([both, diag], axis=1)
        o = jnp.dot(e, both, preferred_element_type=F32)
        outs.append((o[:, :128] / o[:, 128:]).astype(BF16))
    return outs


def halves(width):
    return lax.broadcasted_iota(jnp.int32, (1, 8, width), 1) < 4


def to_quads(cells):
    n, _, width = cells.shape
    pairs = cells.reshape(n // 2, 2, 8, width)
    even, odd = pairs[:, 0], pairs[:, 1]
    left = jnp.where(halves(width), even, pltpu.roll(odd, 4, 1))
    right = jnp.where(halves(width), pltpu.roll(even, 4, 1), odd)
    return left, right


def from_quads(left, right):
    n, _, width = left.shape
    even = jnp.where(halves(width), left, pltpu.roll(right, 4, 1))
    odd = jnp.where(halves(width), pltpu.roll(left, 4, 1), right)
    return jnp.stack([even, odd], axis=1).reshape(2 * n, 8, width)


def window_quads(cells):
    width = cells.shape[-1]
    left, right = to_quads(cells)
    both = [side.reshape(2, QUAD, width) for side in (left, right)]
    return jnp.stack(both, axis=1)


def natural_of_quad(shape, axis):
    n = lax.broadcasted_iota(jnp.int32, shape, axis)
    u, v, r, c = (n >> 5) & 1, (n >> 4) & 1, (n >> 2) & 3, n & 3
    return (u * 4 + r) * 8 + v * 4 + c


def kernel(
    field, w_qkv, w_proj, gains, pos_bias, out,
    x, xq, wqkv, wproj, gain, bias, bias0, bias1, normed, nquad, q0, kv0, ext, q1, kv1, ctx,
    load_sem, out_sem, send_sem, recv_sem,
):
    lat, lon = lax.axis_index("lat"), lax.axis_index("lon")
    n_lat, n_lon = lax.axis_size("lat"), lax.axis_size("lon")

    def partner(dy, dx):
        return {"lat": lax.rem(lat + dy + n_lat, n_lat), "lon": lax.rem(lon + dx + n_lon, n_lon)}

    def inside(dy):
        return (lat + dy >= 0) & (lat + dy < n_lat)

    odd = lax.rem(lat, 2)
    order = (odd, 1 - odd)

    barrier = pltpu.get_barrier_semaphore()
    for dy, dx in PEERS:
        pl.when(inside(dy))(lambda: pl.semaphore_signal(
            barrier, inc=1, device_id=partner(dy, dx), device_id_type=MESH))

    loads = []

    def load(src, dst):
        copy = pltpu.make_async_copy(src, dst, load_sem.at[len(loads)])
        loads.append(copy)
        return copy

    ld_x = load(field, x)
    ld_gain = load(gains, gain)
    ld_qkv = [
        [load(w_qkv.at[s, :, pl.ds(D * c, D)], wqkv.at[s, :, pl.ds(D * c, D)]) for c in range(3)]
        for s in range(2)
    ]
    ld_bias = [load(pos_bias.at[s], bias.at[s]) for s in range(2)]
    ld_proj = [load(w_proj.at[s], wproj.at[s]) for s in range(2)]
    for copy in [ld_x, ld_gain, *ld_qkv[0], ld_bias[0], ld_proj[0]]:
        copy.start()

    ld_x.wait()
    ld_gain.wait()
    for i in range(2):
        for j in range(2):
            w = 2 * i + j
            quads = (slice(2 * i, 2 * i + 2), slice(2 * j, 2 * j + 2))
            cells = x[8 * i:8 * i + 8, 8 * j:8 * j + 8, :]
            unit = layer_norm(cells, gain[0:1, :])
            normed[WIN * w:WIN * w + WIN, :] = unit.reshape(WIN, D).astype(BF16)
            nquad[quads] = window_quads(unit).astype(BF16)
            xq[quads] = window_quads(cells)
    ld_qkv[0][0].wait()
    part = jnp.dot(nquad[...].reshape(256, D), wqkv[0, :, :D], preferred_element_type=F32) * 0.125
    q0[...] = part.astype(BF16).reshape(4, 4, QUAD, D)
    for c in range(2):
        ld_qkv[0][1 + c].wait()
        part = jnp.dot(
            normed[...], wqkv[0, :, D + D * c:2 * D + D * c], preferred_element_type=F32
        )
        kv0[:, :, D * c:D * c + D] = part.astype(BF16).reshape(4, WIN, D)
    ld_bias[0].wait()

    def pair_bias(s, p):
        b = jnp.concatenate([bias[s, 2 * p], bias[s, 2 * p + 1]], axis=1)
        return window_quads(b.reshape(8, 8, 128)).reshape(WIN, 128)

    for p in range(PAIRS):
        bias0[p] = pair_bias(0, p)

    waves = ([], [])

    def send(wave, dy, dx, src, dst):
        n = WAVE * wave + len(waves[wave])
        copy = pltpu.make_async_remote_copy(
            src_ref=ext.at[src],
            dst_ref=ext.at[dst],
            send_sem=send_sem.at[n],
            recv_sem=recv_sem.at[n],
            device_id=partner(dy, dx),
            device_id_type=MESH,
        )
        waves[wave].append(copy)
        return copy

    for wave, i in enumerate(order):
        band = pl.ds(2 * i, 2)
        jobs = [(j, p) for j in range(2) for p in range(PAIRS)]
        quads = [(band, slice(2 * j, 2 * j + 2), slice(None)) for j in range(2)]
        cols = [slice(128 * p, 128 * p + 128) for p in range(PAIRS)]
        outs = attend(
            [q0[(*quads[j], cols[p])].reshape(WIN, 128) for j, p in jobs],
            [kv0[pl.ds(2 * i + j, 1), :, cols[p]].reshape(WIN, 128) for j, p in jobs],
            [kv0[pl.ds(2 * i + j, 1), :, D + 128 * p:D + 128 * p + 128].reshape(WIN, 128) for j, p in jobs],
            [bias0[p] for j, p in jobs],
        )
        for (j, p), o in zip(jobs, outs):
            ctx[(*quads[j], cols[p])] = o.reshape(2, 2, QUAD, 128)
        if wave == 0:
            ld_proj[0].wait()
            for copy in [*ld_qkv[1], ld_bias[1], ld_proj[1]]:
                copy.start()
        update = jnp.dot(ctx[band].reshape(128, D), wproj[0], preferred_element_type=F32)
        cells = xq[band].reshape(128, D) + update
        xq[band] = cells.reshape(2, 4, QUAD, D)
        unit = layer_norm(cells, gain[1:2, :]).astype(BF16)
        ext[pl.ds(1 + 2 * i, 2), OWN] = unit.reshape(2, 4, QUAD, D)
        if wave == 0:
            inner = (lat > 0) & (lat < n_lat - 1)
            pl.when(inner)(lambda: pl.semaphore_wait(barrier, 8))
            pl.when(jnp.logical_not(inner))(lambda: pl.semaphore_wait(barrier, 5))
        half = pl.ds(1 + 2 * i, 2)
        send(wave, 0, -1, (half, slice(1, 2)), (half, slice(5, 6))).start()
        send(wave, 0, 1, (half, slice(4, 5)), (half, slice(0, 1))).start()
        dy = 2 * i - 1
        here, there = pl.ds(1 + 3 * i, 1), pl.ds(5 - 5 * i, 1)
        outward = (
            send(wave, dy, 0, (here, slice(1, 5)), (there, slice(1, 5))),
            send(wave, dy, -1, (here, slice(1, 2)), (there, slice(5, 6))),
            send(wave, dy, 1, (here, slice(4, 5)), (there, slice(0, 1))),
        )

        @pl.when(inside(dy))
        def _():
            for copy in outward:
                copy.start()

    for copy in ld_qkv[1]:
        copy.wait()
    own = ext[OWN, OWN].reshape(256, D)
    own_q = jnp.dot(own, wqkv[1, :, :D], preferred_element_type=F32) * 0.125
    q1[...] = own_q.astype(BF16).reshape(4, 4, QUAD, D)
    own_kv = jnp.dot(own, wqkv[1, :, D:], preferred_element_type=F32)
    kv1[OWN, OWN] = own_kv.astype(BF16).reshape(4, 4, QUAD, 2 * D)
    ld_bias[1].wait()
    ld_proj[1].wait()
    row = lax.broadcasted_iota(jnp.int32, (128, 128), 0)
    lane = lax.broadcasted_iota(jnp.int32, (128, 128), 1)
    key_order = (natural_of_quad((128, 128), 1) + (lane & 64) == row).astype(F32)
    for p in range(PAIRS):
        b = jnp.dot(
            pair_bias(1, p), key_order, precision=lax.Precision.HIGHEST, preferred_element_type=F32
        )
        bias1[p] = b.reshape(2, 2, QUAD, 128)

    @pl.when(lat == 0)
    def _():
        ext[0] = jnp.zeros((6, QUAD, D), BF16)

    @pl.when(lat == n_lat - 1)
    def _():
        ext[5] = jnp.zeros((6, QUAD, D), BF16)

    north = (lax.broadcasted_iota(jnp.int32, (1, 128), 1) & 63) < 32

    def shifted(group):
        qs, ks, vs, biases, places = [], [], [], [], []
        for r0, nr, u0, k0, b, closed in group:
            c0, c1 = max(2 * b - 1, 0), min(2 * b, 3) + 1
            v0, nc = c0 - (2 * b - 1), c1 - c0
            count = nr * nc * QUAD
            here = (pl.ds(k0, 2), slice(2 * b, 2 * b + 2), slice(None))
            for p in range(PAIRS):
                col = slice(128 * p, 128 * p + 128)
                place = (pl.ds(r0, nr), slice(c0, c1), slice(None), col)
                part = bias1[p:p + 1, pl.ds(u0, nr), v0:v0 + nc].reshape(count, 128)
                biases.append(part if closed is None else part + closed)
                qs.append(q1[place].reshape(count, 128))
                ks.append(kv1[(*here, col)].reshape(WIN, 128))
                vs.append(kv1[(*here, slice(D + 128 * p, D + 128 * p + 128))].reshape(WIN, 128))
                places.append((place, (nr, nc, QUAD, 128)))
        for (place, shape), o in zip(places, attend(qs, ks, vs, biases)):
            ctx[place] = o.reshape(shape)

    middle = [(1, 2, 0, 2, b, None) for b in range(3)]

    def edge(i):
        shut = jnp.where(inside(2 * i - 1), 0.0, -1e30)
        closed = jnp.where(north, jnp.where(i == 0, shut, 0.0), jnp.where(i == 1, shut, 0.0))
        return [(3 * i, 1, 1 - i, 4 * i, b, closed) for b in range(3)]

    def halo_kv(units):
        return jnp.dot(units, wqkv[1, :, D:], preferred_element_type=F32).astype(BF16)


    def finish(bands):
        block = jnp.concatenate([ctx[r].reshape(WIN, D) for r in bands], axis=0)
        update = jnp.dot(block, wproj[1], preferred_element_type=F32)
        for n, r in enumerate(bands):
            cells = xq[r] + update[WIN * n:WIN * n + WIN].reshape(4, QUAD, D)
            for j in range(2):
                left, right = [cells[2 * j + v].reshape(2, 8, D) for v in range(2)]
                out[4 * r:4 * r + 4, 8 * j:8 * j + 8, :] = from_quads(left, right)

    shifted([middle[1]])
    for wave in range(2):
        for copy in waves[wave][:2]:
            copy.wait_recv()

    def edge_arrived(wave):
        @pl.when(inside(2 * order[wave] - 1))
        def _():
            for copy in waves[wave][2:]:
                copy.wait_recv()

    edge_arrived(0)
    far = 5 * order[0]
    units = jnp.concatenate(
        [ext[OWN, 0].reshape(64, D), ext[OWN, 5].reshape(64, D), ext[far].reshape(96, D)], axis=0
    )
    got = halo_kv(units)
    kv1[OWN, 0] = got[:64].reshape(4, QUAD, 2 * D)
    kv1[OWN, 5] = got[64:128].reshape(4, QUAD, 2 * D)
    kv1[far] = got[128:].reshape(6, QUAD, 2 * D)
    shifted([middle[0], middle[2], *edge(order[0])])
    finish([1, 2])
    edge_arrived(1)
    far = 5 * order[1]
    kv1[far] = halo_kv(ext[far].reshape(96, D)).reshape(6, QUAD, 2 * D)
    shifted(edge(order[1]))
    finish([0, 3])
    for wave in range(2):
        for copy in waves[wave][:2]:
            copy.wait_send()

        @pl.when(inside(2 * order[wave] - 1))
        def _():
            for copy in waves[wave][2:]:
                copy.wait_send()


def on_device(field, w_qkv, w_proj, norm_gain, pos_bias):
    rows, cols, width = field.shape
    any_space = pl.BlockSpec(memory_space=pl.ANY)
    vmem = pltpu.VMEM
    return pl.pallas_call(
        kernel,
        out_shape=jax.ShapeDtypeStruct(field.shape, F32),
        in_specs=[any_space] * 5,
        out_specs=pl.BlockSpec(memory_space=pltpu.VMEM),
        scratch_shapes=[
            vmem((rows, cols, D), F32),
            vmem((4, 4, QUAD, D), F32),
            vmem((2, D, 3 * D), BF16),
            vmem((2, D, D), BF16),
            vmem((2, D), F32),
            vmem((2, HEADS, WIN, WIN), F32),
            vmem((PAIRS, WIN, 128), F32),
            vmem((PAIRS, 2, 2, QUAD, 128), F32),
            vmem((256, D), BF16),
            vmem((4, 4, QUAD, D), BF16),
            vmem((4, 4, QUAD, D), BF16),
            vmem((4, WIN, 2 * D), BF16),
            vmem((6, 6, QUAD, D), BF16),
            vmem((4, 4, QUAD, D), BF16),
            vmem((6, 6, QUAD, 2 * D), BF16),
            vmem((4, 4, QUAD, D), BF16),
            pltpu.SemaphoreType.DMA((12,)),
            pltpu.SemaphoreType.DMA((4,)),
            pltpu.SemaphoreType.DMA((2 * WAVE,)),
            pltpu.SemaphoreType.DMA((2 * WAVE,)),
        ],
        compiler_params=pltpu.CompilerParams(
            collective_id=0, has_side_effects=True, vmem_limit_bytes=48 * 1024 * 1024
        ),
        cost_estimate=pl.CostEstimate(
            flops=3_300_000_000, bytes_accessed=13_000_000, transcendentals=400_000
        ),
        name="swin_pair",
    )(*[pltpu.with_memory_space_constraint(a, pltpu.HBM) for a in (field, w_qkv, w_proj, norm_gain, pos_bias)])


def solution(mesh):
    return jax.shard_map(
        on_device,
        mesh=mesh,
        in_specs=(P("lat", "lon", None), P(), P(), P(), P()),
        out_specs=P("lat", "lon", None),
        check_vma=False,
    )
```

```python
import functools

import jax
import jax.numpy as jnp
from jax import lax
from jax.experimental import pallas as pl
from jax.experimental.pallas import tpu as pltpu
from jax.sharding import PartitionSpec as P

D = 768
HEADS = 12
PAIRS = HEADS // 2
WIN = 64
QUAD = 16
F32 = jnp.float32
BF16 = jnp.bfloat16
MESH = pl.DeviceIdType.MESH
NT = (((1,), (1,)), ((), ()))

OWN = slice(1, 5)
WAVE = 6


def layer_norm(x, gain):
    mean = jnp.mean(x, axis=-1, keepdims=True)
    centred = x - mean
    var = jnp.mean(centred * centred, axis=-1, keepdims=True)
    return centred * lax.rsqrt(var + 1e-05) * gain


def lanes_low(shape, axis):
    return lax.broadcasted_iota(jnp.int32, shape, axis) < 64


def attend(qs, ks, vs, biases):
    low = lanes_low((1, 128), 1)
    keep0 = low.astype(F32).astype(BF16)
    keep1 = (1.0 - low.astype(F32)).astype(BF16)
    diag = (lanes_low((128, 128), 0) == lanes_low((128, 128), 1)).astype(F32).astype(BF16)
    scores = []
    for q, k, bias in zip(qs, ks, biases):
        both = jnp.concatenate([k * keep0, k * keep1], axis=0)
        scores.append(lax.dot_general(q, both, NT, preferred_element_type=F32) + bias)
    tops = []
    for s in scores:
        top0 = jnp.max(jnp.where(low, s, -jnp.inf), axis=-1, keepdims=True)
        top1 = jnp.max(jnp.where(low, -jnp.inf, s), axis=-1, keepdims=True)
        tops.append(jnp.where(low, top0, top1))
    expos = [jnp.exp(s - top).astype(BF16) for s, top in zip(scores, tops)]
    outs = []
    for e, v in zip(expos, vs):
        both = jnp.concatenate([v * keep0, v * keep1], axis=0)
        both = jnp.concatenate([both, diag], axis=1)
        o = jnp.dot(e, both, preferred_element_type=F32)
        outs.append((o[:, :128] / o[:, 128:]).astype(BF16))
    return outs


def halves(width):
    return lax.broadcasted_iota(jnp.int32, (1, 8, width), 1) < 4


def to_quads(cells):
    n, _, width = cells.shape
    pairs = cells.reshape(n // 2, 2, 8, width)
    even, odd = pairs[:, 0], pairs[:, 1]
    left = jnp.where(halves(width), even, pltpu.roll(odd, 4, 1))
    right = jnp.where(halves(width), pltpu.roll(even, 4, 1), odd)
    return left, right


def from_quads(left, right):
    n, _, width = left.shape
    even = jnp.where(halves(width), left, pltpu.roll(right, 4, 1))
    odd = jnp.where(halves(width), pltpu.roll(left, 4, 1), right)
    return jnp.stack([even, odd], axis=1).reshape(2 * n, 8, width)


def window_quads(cells):
    width = cells.shape[-1]
    left, right = to_quads(cells)
    both = [side.reshape(2, QUAD, width) for side in (left, right)]
    return jnp.stack(both, axis=1)


def natural_of_quad(shape, axis):
    n = lax.broadcasted_iota(jnp.int32, shape, axis)
    u, v, r, c = (n >> 5) & 1, (n >> 4) & 1, (n >> 2) & 3, n & 3
    return (u * 4 + r) * 8 + v * 4 + c


def kernel(
    field, w_qkv, w_proj, gains, pos_bias, out,
    x, xq, wqkv, wproj, gain, bias, bias0, bias1, normed, nquad, q0, kv0, ext, q1, kv1, ctx,
    load_sem, out_sem, send_sem, recv_sem,
):
    lat, lon = lax.axis_index("lat"), lax.axis_index("lon")
    n_lat, n_lon = lax.axis_size("lat"), lax.axis_size("lon")

    def partner(dy, dx):
        return {"lat": lax.rem(lat + dy + n_lat, n_lat), "lon": lax.rem(lon + dx + n_lon, n_lon)}

    def inside(dy):
        return (lat + dy >= 0) & (lat + dy < n_lat)

    odd = lax.rem(lat, 2)
    order = (odd, 1 - odd)

    core = lax.rem(lon, 2)
    outside = 2 * core - 1

    barrier = pltpu.get_barrier_semaphore()
    for dy, dx in ((0, -1), (0, 1), (-1, 0), (1, 0), (-1, outside), (1, outside)):
        pl.when(inside(dy))(lambda: pl.semaphore_signal(
            barrier, inc=1, device_id=partner(dy, dx), device_id_type=MESH))

    loads = []

    def load(src, dst):
        copy = pltpu.make_async_copy(src, dst, load_sem.at[len(loads)])
        loads.append(copy)
        return copy

    ld_x = load(field, x)
    ld_gain = load(gains, gain)
    ld_qkv = [
        [load(w_qkv.at[s, :, pl.ds(D * c, D)], wqkv.at[s, :, pl.ds(D * c, D)]) for c in range(3)]
        for s in range(2)
    ]
    ld_bias = [load(pos_bias.at[s], bias.at[s]) for s in range(2)]
    ld_proj = [load(w_proj.at[s], wproj.at[s]) for s in range(2)]
    for copy in [ld_x, ld_gain, *ld_qkv[0], ld_bias[0], ld_proj[0]]:
        copy.start()

    ld_x.wait()
    ld_gain.wait()
    for i in range(2):
        for j in range(2):
            w = 2 * i + j
            quads = (slice(2 * i, 2 * i + 2), slice(2 * j, 2 * j + 2))
            cells = x[8 * i:8 * i + 8, 8 * j:8 * j + 8, :]
            unit = layer_norm(cells, gain[0:1, :])
            normed[w] = unit.reshape(WIN, D).astype(BF16)
            nquad[quads] = window_quads(unit).astype(BF16)
            xq[quads] = window_quads(cells)
    ld_qkv[0][0].wait()
    part = jnp.dot(nquad[...].reshape(256, D), wqkv[0, :, :D], preferred_element_type=F32) * 0.125
    q0[...] = part.astype(BF16).reshape(4, 4, QUAD, D)
    ld_qkv[0][1].wait()
    part = jnp.dot(normed[...].reshape(256, D), wqkv[0, :, D:2 * D], preferred_element_type=F32)
    kv0[:, :, :D] = part.astype(BF16).reshape(4, WIN, D)
    ld_bias[0].wait()

    def pair_bias(s, p):
        b = jnp.concatenate([bias[s, 2 * p], bias[s, 2 * p + 1]], axis=1)
        return window_quads(b.reshape(8, 8, 128)).reshape(WIN, 128)

    for p in range(PAIRS):
        bias0[p] = pair_bias(0, p)

    waves = ([], [])

    def send(wave, dy, dx, src, dst):
        n = WAVE * wave + len(waves[wave])
        copy = pltpu.make_async_remote_copy(
            src_ref=ext.at[src],
            dst_ref=ext.at[dst],
            send_sem=send_sem.at[n],
            recv_sem=recv_sem.at[n],
            device_id=partner(dy, dx),
            device_id_type=MESH,
        )
        waves[wave].append(copy)
        return copy

    for wave, i in enumerate(order):
        band = pl.ds(2 * i, 2)
        pair = pl.ds(2 * i, 2)
        if wave == 0:
            ld_qkv[0][2].wait()
        part = jnp.dot(
            normed[pair].reshape(128, D), wqkv[0, :, 2 * D:], preferred_element_type=F32
        )
        kv0[pair, :, D:] = part.astype(BF16).reshape(2, WIN, D)
        jobs = [(j, p) for j in range(2) for p in range(PAIRS)]
        quads = [(band, slice(2 * j, 2 * j + 2), slice(None)) for j in range(2)]
        cols = [slice(128 * p, 128 * p + 128) for p in range(PAIRS)]
        outs = attend(
            [q0[(*quads[j], cols[p])].reshape(WIN, 128) for j, p in jobs],
            [kv0[pl.ds(2 * i + j, 1), :, cols[p]].reshape(WIN, 128) for j, p in jobs],
            [kv0[pl.ds(2 * i + j, 1), :, D + 128 * p:D + 128 * p + 128].reshape(WIN, 128) for j, p in jobs],
            [bias0[p] for j, p in jobs],
        )
        for (j, p), o in zip(jobs, outs):
            ctx[(*quads[j], cols[p])] = o.reshape(2, 2, QUAD, 128)
        if wave == 0:
            ld_proj[0].wait()
            for copy in [*ld_qkv[1], ld_bias[1], ld_proj[1]]:
                copy.start()
        update = jnp.dot(ctx[band].reshape(128, D), wproj[0], preferred_element_type=F32)
        cells = xq[band].reshape(128, D) + update
        xq[band] = cells.reshape(2, 4, QUAD, D)
        unit = layer_norm(cells, gain[1:2, :]).astype(BF16)
        ext[pl.ds(1 + 2 * i, 2), OWN] = unit.reshape(2, 4, QUAD, D)
        if wave == 0:
            inner = (lat > 0) & (lat < n_lat - 1)
            pl.when(inner)(lambda: pl.semaphore_wait(barrier, 6))
            pl.when(jnp.logical_not(inner))(lambda: pl.semaphore_wait(barrier, 4))
        half = pl.ds(1 + 2 * i, 2)
        dy = 2 * i - 1
        here, there = pl.ds(1 + 3 * i, 1), pl.ds(5 - 5 * i, 1)
        shared, rest = pl.ds(4 - 3 * core, 1), pl.ds(1 + core, 3)
        west = send(wave, 0, -1, (half, slice(1, 2)), (half, slice(5, 6)))
        east = send(wave, 0, 1, (half, slice(4, 5)), (half, slice(0, 1)))
        first = send(wave, dy, 0, (here, shared), (there, shared))
        outward = (
            send(wave, dy, 0, (here, rest), (there, rest)),
            send(wave, dy, outside, (here, pl.ds(1 + 3 * core, 1)), (there, pl.ds(5 - 5 * core, 1))),
        )
        far = pl.ds(5 * i, 1)
        send(wave, 0, -outside, (far, shared), (far, pl.ds(5 * core, 1)))
        pl.when(inside(dy))(first.start)
        west.start()
        east.start()

        @pl.when(inside(dy))
        def _():
            for copy in outward:
                copy.start()

    for copy in ld_qkv[1]:
        copy.wait()
    own = ext[OWN, OWN].reshape(256, D)
    own_q = jnp.dot(own, wqkv[1, :, :D], preferred_element_type=F32) * 0.125
    q1[...] = own_q.astype(BF16).reshape(4, 4, QUAD, D)
    own_kv = jnp.dot(own, wqkv[1, :, D:], preferred_element_type=F32)
    kv1[OWN, OWN] = own_kv.astype(BF16).reshape(4, 4, QUAD, 2 * D)
    ld_bias[1].wait()
    ld_proj[1].wait()
    row = lax.broadcasted_iota(jnp.int32, (128, 128), 0)
    lane = lax.broadcasted_iota(jnp.int32, (128, 128), 1)
    key_order = (natural_of_quad((128, 128), 1) + (lane & 64) == row).astype(F32)
    for p in range(PAIRS):
        b = jnp.dot(
            pair_bias(1, p), key_order, precision=lax.Precision.HIGHEST, preferred_element_type=F32
        )
        bias1[p] = b.reshape(2, 2, QUAD, 128)

    @pl.when(lat == 0)
    def _():
        ext[0] = jnp.zeros((6, QUAD, D), BF16)

    @pl.when(lat == n_lat - 1)
    def _():
        ext[5] = jnp.zeros((6, QUAD, D), BF16)

    north = (lax.broadcasted_iota(jnp.int32, (1, 128), 1) & 63) < 32

    def shifted(group):
        qs, ks, vs, biases, places = [], [], [], [], []
        for r0, nr, u0, k0, b, closed in group:
            c0, c1 = max(2 * b - 1, 0), min(2 * b, 3) + 1
            v0, nc = c0 - (2 * b - 1), c1 - c0
            count = nr * nc * QUAD
            here = (pl.ds(k0, 2), slice(2 * b, 2 * b + 2), slice(None))
            for p in range(PAIRS):
                col = slice(128 * p, 128 * p + 128)
                place = (pl.ds(r0, nr), slice(c0, c1), slice(None), col)
                part = bias1[p:p + 1, pl.ds(u0, nr), v0:v0 + nc].reshape(count, 128)
                biases.append(part if closed is None else part + closed)
                qs.append(q1[place].reshape(count, 128))
                ks.append(kv1[(*here, col)].reshape(WIN, 128))
                vs.append(kv1[(*here, slice(D + 128 * p, D + 128 * p + 128))].reshape(WIN, 128))
                places.append((place, (nr, nc, QUAD, 128)))
        for (place, shape), o in zip(places, attend(qs, ks, vs, biases)):
            ctx[place] = o.reshape(shape)

    middle = [(1, 2, 0, 2, b, None) for b in range(3)]

    def edge(i):
        shut = jnp.where(inside(2 * i - 1), 0.0, -1e30)
        closed = jnp.where(north, jnp.where(i == 0, shut, 0.0), jnp.where(i == 1, shut, 0.0))
        return [(3 * i, 1, 1 - i, 4 * i, b, closed) for b in range(3)]

    def halo_kv(units):
        return jnp.dot(units, wqkv[1, :, D:], preferred_element_type=F32).astype(BF16)


    def finish(bands):
        block = jnp.concatenate([ctx[pl.ds(r, 1)].reshape(WIN, D) for r in bands], axis=0)
        update = jnp.dot(block, wproj[1], preferred_element_type=F32)
        for n, r in enumerate(bands):
            cells = xq[pl.ds(r, 1)].reshape(4, QUAD, D)
            cells = cells + update[WIN * n:WIN * n + WIN].reshape(4, QUAD, D)
            for j in range(2):
                left, right = [cells[2 * j + v].reshape(2, 8, D) for v in range(2)]
                out[pl.ds(4 * r, 4), 8 * j:8 * j + 8, :] = from_quads(left, right)

    def pass_on(wave):
        @pl.when(inside(2 * order[wave] - 1))
        def _():
            waves[wave][2].wait_recv()
            waves[wave][5].start()

    pass_on(0)
    shifted([middle[1]])
    pass_on(1)
    def sides_arrived(wave):
        for copy in waves[wave][:2]:
            copy.wait_recv()

    def edge_arrived(wave):
        @pl.when(inside(2 * order[wave] - 1))
        def _():
            for copy in waves[wave][3:]:
                copy.wait_recv()

    def side_units(wave):
        half = pl.ds(1 + 2 * order[wave], 2)
        return [ext[half, c:c + 1].reshape(32, D) for c in (0, 5)]

    def side_kv(wave, got):
        half = pl.ds(1 + 2 * order[wave], 2)
        for n, c in enumerate((0, 5)):
            kv1[half, c:c + 1] = got[32 * n:32 * n + 32].reshape(2, 1, QUAD, 2 * D)

    sides_arrived(0)
    edge_arrived(0)
    far = 5 * order[0]
    got = halo_kv(jnp.concatenate([*side_units(0), ext[far].reshape(96, D)], axis=0))
    side_kv(0, got)
    kv1[far] = got[64:].reshape(6, QUAD, 2 * D)
    shifted(edge(order[0]))
    sides_arrived(1)
    side_kv(1, halo_kv(jnp.concatenate(side_units(1), axis=0)))
    shifted([middle[0], middle[2]])
    finish([1, 2, 3 * order[0]])
    edge_arrived(1)
    far = 5 * order[1]
    kv1[far] = halo_kv(ext[far].reshape(96, D)).reshape(6, QUAD, 2 * D)
    shifted(edge(order[1]))
    finish([3 * order[1]])
    for wave in range(2):
        for copy in waves[wave][:2]:
            copy.wait_send()

        @pl.when(inside(2 * order[wave] - 1))
        def _():
            for copy in waves[wave][2:]:
                copy.wait_send()


def on_device(field, w_qkv, w_proj, norm_gain, pos_bias):
    rows, cols, width = field.shape
    any_space = pl.BlockSpec(memory_space=pl.ANY)
    vmem = pltpu.VMEM
    return pl.pallas_call(
        kernel,
        out_shape=jax.ShapeDtypeStruct(field.shape, F32),
        in_specs=[any_space] * 5,
        out_specs=pl.BlockSpec(memory_space=pltpu.VMEM),
        scratch_shapes=[
            vmem((rows, cols, D), F32),
            vmem((4, 4, QUAD, D), F32),
            vmem((2, D, 3 * D), BF16),
            vmem((2, D, D), BF16),
            vmem((2, D), F32),
            vmem((2, HEADS, WIN, WIN), F32),
            vmem((PAIRS, WIN, 128), F32),
            vmem((PAIRS, 2, 2, QUAD, 128), F32),
            vmem((4, WIN, D), BF16),
            vmem((4, 4, QUAD, D), BF16),
            vmem((4, 4, QUAD, D), BF16),
            vmem((4, WIN, 2 * D), BF16),
            vmem((6, 6, QUAD, D), BF16),
            vmem((4, 4, QUAD, D), BF16),
            vmem((6, 6, QUAD, 2 * D), BF16),
            vmem((4, 4, QUAD, D), BF16),
            pltpu.SemaphoreType.DMA((12,)),
            pltpu.SemaphoreType.DMA((4,)),
            pltpu.SemaphoreType.DMA((2 * WAVE,)),
            pltpu.SemaphoreType.DMA((2 * WAVE,)),
        ],
        compiler_params=pltpu.CompilerParams(
            collective_id=0, has_side_effects=True, vmem_limit_bytes=48 * 1024 * 1024
        ),
        cost_estimate=pl.CostEstimate(
            flops=3_300_000_000, bytes_accessed=13_000_000, transcendentals=400_000
        ),
        name="swin_pair",
    )(*[pltpu.with_memory_space_constraint(a, pltpu.HBM) for a in (field, w_qkv, w_proj, norm_gain, pos_bias)])


def solution(mesh):
    return jax.shard_map(
        on_device,
        mesh=mesh,
        in_specs=(P("lat", "lon", None), P(), P(), P(), P()),
        out_specs=P("lat", "lon", None),
        check_vma=False,
    )
```

```python
import functools

import jax
import jax.numpy as jnp
from jax import lax
from jax.experimental import pallas as pl
from jax.experimental.pallas import tpu as pltpu
from jax.sharding import PartitionSpec as P

D = 768
HEADS = 12
PAIRS = HEADS // 2
WIN = 64
QUAD = 16
F32 = jnp.float32
BF16 = jnp.bfloat16
MESH = pl.DeviceIdType.MESH
NT = (((1,), (1,)), ((), ()))

OWN = slice(1, 5)
WAVE = 6


def layer_norm(x, gain):
    mean = jnp.mean(x, axis=-1, keepdims=True)
    centred = x - mean
    var = jnp.mean(centred * centred, axis=-1, keepdims=True)
    return centred * lax.rsqrt(var + 1e-05) * gain


def lanes_low(shape, axis):
    return lax.broadcasted_iota(jnp.int32, shape, axis) < 64


def attend(qs, ks, vs, biases):
    low = lanes_low((1, 128), 1)
    keep0 = low.astype(F32).astype(BF16)
    keep1 = (1.0 - low.astype(F32)).astype(BF16)
    diag = (lanes_low((128, 128), 0) == lanes_low((128, 128), 1)).astype(F32).astype(BF16)
    scores = []
    for q, k, bias in zip(qs, ks, biases):
        both = jnp.concatenate([k * keep0, k * keep1], axis=0)
        scores.append(lax.dot_general(q, both, NT, preferred_element_type=F32) + bias)
    tops = []
    for s in scores:
        top0 = jnp.max(jnp.where(low, s, -jnp.inf), axis=-1, keepdims=True)
        top1 = jnp.max(jnp.where(low, -jnp.inf, s), axis=-1, keepdims=True)
        tops.append(jnp.where(low, top0, top1))
    expos = [jnp.exp(s - top).astype(BF16) for s, top in zip(scores, tops)]
    outs = []
    for e, v in zip(expos, vs):
        both = jnp.concatenate([v * keep0, v * keep1], axis=0)
        both = jnp.concatenate([both, diag], axis=1)
        o = jnp.dot(e, both, preferred_element_type=F32)
        outs.append((o[:, :128] / o[:, 128:]).astype(BF16))
    return outs


def halves(width):
    return lax.broadcasted_iota(jnp.int32, (1, 8, width), 1) < 4


def to_quads(cells):
    n, _, width = cells.shape
    pairs = cells.reshape(n // 2, 2, 8, width)
    even, odd = pairs[:, 0], pairs[:, 1]
    left = jnp.where(halves(width), even, pltpu.roll(odd, 4, 1))
    right = jnp.where(halves(width), pltpu.roll(even, 4, 1), odd)
    return left, right


def from_quads(left, right):
    n, _, width = left.shape
    even = jnp.where(halves(width), left, pltpu.roll(right, 4, 1))
    odd = jnp.where(halves(width), pltpu.roll(left, 4, 1), right)
    return jnp.stack([even, odd], axis=1).reshape(2 * n, 8, width)


def window_quads(cells):
    width = cells.shape[-1]
    left, right = to_quads(cells)
    both = [side.reshape(2, QUAD, width) for side in (left, right)]
    return jnp.stack(both, axis=1)


def natural_of_quad(shape, axis):
    n = lax.broadcasted_iota(jnp.int32, shape, axis)
    u, v, r, c = (n >> 5) & 1, (n >> 4) & 1, (n >> 2) & 3, n & 3
    return (u * 4 + r) * 8 + v * 4 + c


def kernel(
    field, w_qkv, w_proj, gains, pos_bias, out,
    x, xq, wqkv, wproj, gain, bias, bias0, bias1, normed, nquad, q0, kv0, ext, q1, kv1, ctx,
    load_sem, out_sem, send_sem, recv_sem,
):
    lat, lon = lax.axis_index("lat"), lax.axis_index("lon")
    n_lat, n_lon = lax.axis_size("lat"), lax.axis_size("lon")

    def partner(dy, dx):
        return {"lat": lax.rem(lat + dy + n_lat, n_lat), "lon": lax.rem(lon + dx + n_lon, n_lon)}

    def inside(dy):
        return (lat + dy >= 0) & (lat + dy < n_lat)

    odd = lax.rem(lat, 2)
    order = (odd, 1 - odd)

    core = lax.rem(lon, 2)
    outside = 2 * core - 1

    barrier = pltpu.get_barrier_semaphore()
    for dy, dx in ((0, -1), (0, 1), (-1, 0), (1, 0), (-1, outside), (1, outside)):
        pl.when(inside(dy))(lambda: pl.semaphore_signal(
            barrier, inc=1, device_id=partner(dy, dx), device_id_type=MESH))

    loads = []

    def load(src, dst):
        copy = pltpu.make_async_copy(src, dst, load_sem.at[len(loads)])
        loads.append(copy)
        return copy

    ld_x = load(field, x)
    ld_gain = load(gains, gain)
    ld_qkv = [
        [load(w_qkv.at[s, :, pl.ds(D * c, D)], wqkv.at[s, :, pl.ds(D * c, D)]) for c in range(3)]
        for s in range(2)
    ]
    ld_bias = [load(pos_bias.at[s], bias.at[s]) for s in range(2)]
    ld_proj = [load(w_proj.at[s], wproj.at[s]) for s in range(2)]
    for copy in [ld_x, ld_gain, *ld_qkv[0], ld_bias[0], ld_proj[0]]:
        copy.start()

    ld_x.wait()
    ld_gain.wait()
    for i in range(2):
        for j in range(2):
            w = 2 * i + j
            quads = (slice(2 * i, 2 * i + 2), slice(2 * j, 2 * j + 2))
            cells = x[8 * i:8 * i + 8, 8 * j:8 * j + 8, :]
            unit = layer_norm(cells, gain[0:1, :])
            normed[w] = unit.reshape(WIN, D).astype(BF16)
            nquad[quads] = window_quads(unit).astype(BF16)
            xq[quads] = window_quads(cells)
    ld_qkv[0][0].wait()
    part = jnp.dot(nquad[...].reshape(256, D), wqkv[0, :, :D], preferred_element_type=F32) * 0.125
    q0[...] = part.astype(BF16).reshape(4, 4, QUAD, D)
    ld_qkv[0][1].wait()
    part = jnp.dot(normed[...].reshape(256, D), wqkv[0, :, D:2 * D], preferred_element_type=F32)
    kv0[:, :, :D] = part.astype(BF16).reshape(4, WIN, D)
    ld_bias[0].wait()

    def pair_bias(s, p):
        b = jnp.concatenate([bias[s, 2 * p], bias[s, 2 * p + 1]], axis=1)
        return window_quads(b.reshape(8, 8, 128)).reshape(WIN, 128)

    for p in range(PAIRS):
        bias0[p] = pair_bias(0, p)

    waves = ([], [])

    def send(wave, dy, dx, src, dst):
        n = WAVE * wave + len(waves[wave])
        copy = pltpu.make_async_remote_copy(
            src_ref=ext.at[src],
            dst_ref=ext.at[dst],
            send_sem=send_sem.at[n],
            recv_sem=recv_sem.at[n],
            device_id=partner(dy, dx),
            device_id_type=MESH,
        )
        waves[wave].append(copy)
        return copy

    for wave, i in enumerate(order):
        band = pl.ds(2 * i, 2)
        pair = pl.ds(2 * i, 2)
        if wave == 0:
            ld_qkv[0][2].wait()
        part = jnp.dot(
            normed[pair].reshape(128, D), wqkv[0, :, 2 * D:], preferred_element_type=F32
        )
        kv0[pair, :, D:] = part.astype(BF16).reshape(2, WIN, D)
        jobs = [(j, p) for j in range(2) for p in range(PAIRS)]
        quads = [(band, slice(2 * j, 2 * j + 2), slice(None)) for j in range(2)]
        cols = [slice(128 * p, 128 * p + 128) for p in range(PAIRS)]
        outs = attend(
            [q0[(*quads[j], cols[p])].reshape(WIN, 128) for j, p in jobs],
            [kv0[pl.ds(2 * i + j, 1), :, cols[p]].reshape(WIN, 128) for j, p in jobs],
            [kv0[pl.ds(2 * i + j, 1), :, D + 128 * p:D + 128 * p + 128].reshape(WIN, 128) for j, p in jobs],
            [bias0[p] for j, p in jobs],
        )
        for (j, p), o in zip(jobs, outs):
            ctx[(*quads[j], cols[p])] = o.reshape(2, 2, QUAD, 128)
        if wave == 0:
            ld_proj[0].wait()
            for copy in [*ld_qkv[1], ld_bias[1], ld_proj[1]]:
                copy.start()
        update = jnp.dot(ctx[band].reshape(128, D), wproj[0], preferred_element_type=F32)
        cells = xq[band].reshape(128, D) + update
        xq[band] = cells.reshape(2, 4, QUAD, D)
        unit = layer_norm(cells, gain[1:2, :]).astype(BF16)
        ext[pl.ds(1 + 2 * i, 2), OWN] = unit.reshape(2, 4, QUAD, D)
        if wave == 0:
            inner = (lat > 0) & (lat < n_lat - 1)
            pl.when(inner)(lambda: pl.semaphore_wait(barrier, 6))
            pl.when(jnp.logical_not(inner))(lambda: pl.semaphore_wait(barrier, 4))
        half = pl.ds(1 + 2 * i, 2)
        dy = 2 * i - 1
        here, there = pl.ds(1 + 3 * i, 1), pl.ds(5 - 5 * i, 1)
        shared, rest = pl.ds(4 - 3 * core, 1), pl.ds(1 + core, 3)
        west = send(wave, 0, -1, (half, slice(1, 2)), (half, slice(5, 6)))
        east = send(wave, 0, 1, (half, slice(4, 5)), (half, slice(0, 1)))
        first = send(wave, dy, 0, (here, shared), (there, shared))
        outward = (
            send(wave, dy, 0, (here, rest), (there, rest)),
            send(wave, dy, outside, (here, pl.ds(1 + 3 * core, 1)), (there, pl.ds(5 - 5 * core, 1))),
        )
        far = pl.ds(5 * i, 1)
        send(wave, 0, -outside, (far, shared), (far, pl.ds(5 * core, 1)))
        @pl.when(inside(dy))
        def _():
            first.start()
            outward[1].start()

        west.start()
        east.start()
        pl.when(inside(dy))(outward[0].start)

    for copy in ld_qkv[1]:
        copy.wait()
    own = ext[OWN, OWN].reshape(256, D)
    own_q = jnp.dot(own, wqkv[1, :, :D], preferred_element_type=F32) * 0.125
    q1[...] = own_q.astype(BF16).reshape(4, 4, QUAD, D)
    own_kv = jnp.dot(own, wqkv[1, :, D:], preferred_element_type=F32)
    kv1[OWN, OWN] = own_kv.astype(BF16).reshape(4, 4, QUAD, 2 * D)
    ld_bias[1].wait()
    ld_proj[1].wait()
    row = lax.broadcasted_iota(jnp.int32, (128, 128), 0)
    lane = lax.broadcasted_iota(jnp.int32, (128, 128), 1)
    key_order = (natural_of_quad((128, 128), 1) + (lane & 64) == row).astype(F32)
    for p in range(PAIRS):
        b = jnp.dot(
            pair_bias(1, p), key_order, precision=lax.Precision.HIGHEST, preferred_element_type=F32
        )
        bias1[p] = b.reshape(2, 2, QUAD, 128)

    @pl.when(lat == 0)
    def _():
        ext[0] = jnp.zeros((6, QUAD, D), BF16)

    @pl.when(lat == n_lat - 1)
    def _():
        ext[5] = jnp.zeros((6, QUAD, D), BF16)

    north = (lax.broadcasted_iota(jnp.int32, (1, 128), 1) & 63) < 32

    def shifted(group):
        qs, ks, vs, biases, places = [], [], [], [], []
        for r0, nr, u0, k0, b, closed in group:
            c0, c1 = max(2 * b - 1, 0), min(2 * b, 3) + 1
            v0, nc = c0 - (2 * b - 1), c1 - c0
            count = nr * nc * QUAD
            here = (pl.ds(k0, 2), slice(2 * b, 2 * b + 2), slice(None))
            for p in range(PAIRS):
                col = slice(128 * p, 128 * p + 128)
                place = (pl.ds(r0, nr), slice(c0, c1), slice(None), col)
                part = bias1[p:p + 1, pl.ds(u0, nr), v0:v0 + nc].reshape(count, 128)
                biases.append(part if closed is None else part + closed)
                qs.append(q1[place].reshape(count, 128))
                ks.append(kv1[(*here, col)].reshape(WIN, 128))
                vs.append(kv1[(*here, slice(D + 128 * p, D + 128 * p + 128))].reshape(WIN, 128))
                places.append((place, (nr, nc, QUAD, 128)))
        for (place, shape), o in zip(places, attend(qs, ks, vs, biases)):
            ctx[place] = o.reshape(shape)

    middle = [(1, 2, 0, 2, b, None) for b in range(3)]

    def edge(i):
        shut = jnp.where(inside(2 * i - 1), 0.0, -1e30)
        closed = jnp.where(north, jnp.where(i == 0, shut, 0.0), jnp.where(i == 1, shut, 0.0))
        return [(3 * i, 1, 1 - i, 4 * i, b, closed) for b in range(3)]

    def halo_kv(units):
        return jnp.dot(units, wqkv[1, :, D:], preferred_element_type=F32).astype(BF16)


    def finish(bands):
        block = jnp.concatenate([ctx[pl.ds(r, 1)].reshape(WIN, D) for r in bands], axis=0)
        update = jnp.dot(block, wproj[1], preferred_element_type=F32)
        for n, r in enumerate(bands):
            cells = xq[pl.ds(r, 1)].reshape(4, QUAD, D)
            cells = cells + update[WIN * n:WIN * n + WIN].reshape(4, QUAD, D)
            for j in range(2):
                left, right = [cells[2 * j + v].reshape(2, 8, D) for v in range(2)]
                out[pl.ds(4 * r, 4), 8 * j:8 * j + 8, :] = from_quads(left, right)

    def pass_on(wave):
        @pl.when(inside(2 * order[wave] - 1))
        def _():
            waves[wave][2].wait_recv()
            waves[wave][5].start()

    pass_on(0)
    shifted([middle[1]])

    def sides_arrived(wave):
        for copy in waves[wave][:2]:
            copy.wait_recv()

    def edge_arrived(wave):
        @pl.when(inside(2 * order[wave] - 1))
        def _():
            for copy in waves[wave][3:]:
                copy.wait_recv()

    def side_units(wave):
        half = pl.ds(1 + 2 * order[wave], 2)
        return [ext[half, c:c + 1].reshape(32, D) for c in (0, 5)]

    def side_kv(wave, got):
        half = pl.ds(1 + 2 * order[wave], 2)
        for n, c in enumerate((0, 5)):
            kv1[half, c:c + 1] = got[32 * n:32 * n + 32].reshape(2, 1, QUAD, 2 * D)

    sides_arrived(0)
    edge_arrived(0)
    far = 5 * order[0]
    got = halo_kv(jnp.concatenate([*side_units(0), ext[far].reshape(96, D)], axis=0))
    side_kv(0, got)
    kv1[far] = got[64:].reshape(6, QUAD, 2 * D)
    shifted(edge(order[0]))
    pass_on(1)
    sides_arrived(1)
    side_kv(1, halo_kv(jnp.concatenate(side_units(1), axis=0)))
    shifted([middle[0], middle[2]])
    finish([1, 2, 3 * order[0]])
    edge_arrived(1)
    far = 5 * order[1]
    kv1[far] = halo_kv(ext[far].reshape(96, D)).reshape(6, QUAD, 2 * D)
    shifted(edge(order[1]))
    finish([3 * order[1]])
    for wave in range(2):
        for copy in waves[wave][:2]:
            copy.wait_send()

        @pl.when(inside(2 * order[wave] - 1))
        def _():
            for copy in waves[wave][2:]:
                copy.wait_send()


def on_device(field, w_qkv, w_proj, norm_gain, pos_bias):
    rows, cols, width = field.shape
    any_space = pl.BlockSpec(memory_space=pl.ANY)
    vmem = pltpu.VMEM
    return pl.pallas_call(
        kernel,
        out_shape=jax.ShapeDtypeStruct(field.shape, F32),
        in_specs=[any_space] * 5,
        out_specs=pl.BlockSpec(memory_space=pltpu.VMEM),
        scratch_shapes=[
            vmem((rows, cols, D), F32),
            vmem((4, 4, QUAD, D), F32),
            vmem((2, D, 3 * D), BF16),
            vmem((2, D, D), BF16),
            vmem((2, D), F32),
            vmem((2, HEADS, WIN, WIN), F32),
            vmem((PAIRS, WIN, 128), F32),
            vmem((PAIRS, 2, 2, QUAD, 128), F32),
            vmem((4, WIN, D), BF16),
            vmem((4, 4, QUAD, D), BF16),
            vmem((4, 4, QUAD, D), BF16),
            vmem((4, WIN, 2 * D), BF16),
            vmem((6, 6, QUAD, D), BF16),
            vmem((4, 4, QUAD, D), BF16),
            vmem((6, 6, QUAD, 2 * D), BF16),
            vmem((4, 4, QUAD, D), BF16),
            pltpu.SemaphoreType.DMA((12,)),
            pltpu.SemaphoreType.DMA((4,)),
            pltpu.SemaphoreType.DMA((2 * WAVE,)),
            pltpu.SemaphoreType.DMA((2 * WAVE,)),
        ],
        compiler_params=pltpu.CompilerParams(
            collective_id=0, has_side_effects=True, vmem_limit_bytes=48 * 1024 * 1024
        ),
        cost_estimate=pl.CostEstimate(
            flops=3_300_000_000, bytes_accessed=13_000_000, transcendentals=400_000
        ),
        name="swin_pair",
    )(*[pltpu.with_memory_space_constraint(a, pltpu.HBM) for a in (field, w_qkv, w_proj, norm_gain, pos_bias)])


def solution(mesh):
    return jax.shard_map(
        on_device,
        mesh=mesh,
        in_specs=(P("lat", "lon", None), P(), P(), P(), P()),
        out_specs=P("lat", "lon", None),
        check_vma=False,
    )
```

```python
import functools

import jax
import jax.numpy as jnp
from jax import lax
from jax.experimental import pallas as pl
from jax.experimental.pallas import tpu as pltpu
from jax.sharding import PartitionSpec as P

D = 768
HEADS = 12
PAIRS = HEADS // 2
WIN = 64
QUAD = 16
F32 = jnp.float32
BF16 = jnp.bfloat16
MESH = pl.DeviceIdType.MESH
NT = (((1,), (1,)), ((), ()))

OWN = slice(1, 5)
WAVE = 6


def layer_norm(x, gain):
    mean = jnp.mean(x, axis=-1, keepdims=True)
    centred = x - mean
    var = jnp.mean(centred * centred, axis=-1, keepdims=True)
    return centred * lax.rsqrt(var + 1e-05) * gain


def lanes_low(shape, axis):
    return lax.broadcasted_iota(jnp.int32, shape, axis) < 64


def attend(qs, ks, vs, biases):
    low = lanes_low((1, 128), 1)
    keep0 = low.astype(F32).astype(BF16)
    keep1 = (1.0 - low.astype(F32)).astype(BF16)
    diag = (lanes_low((128, 128), 0) == lanes_low((128, 128), 1)).astype(F32).astype(BF16)
    scores = []
    for q, k, bias in zip(qs, ks, biases):
        both = jnp.concatenate([k * keep0, k * keep1], axis=0)
        scores.append(lax.dot_general(q, both, NT, preferred_element_type=F32) + bias)
    tops = []
    for s in scores:
        top0 = jnp.max(jnp.where(low, s, -jnp.inf), axis=-1, keepdims=True)
        top1 = jnp.max(jnp.where(low, -jnp.inf, s), axis=-1, keepdims=True)
        tops.append(jnp.where(low, top0, top1))
    expos = [jnp.exp(s - top).astype(BF16) for s, top in zip(scores, tops)]
    outs = []
    for e, v in zip(expos, vs):
        both = jnp.concatenate([v * keep0, v * keep1], axis=0)
        both = jnp.concatenate([both, diag], axis=1)
        o = jnp.dot(e, both, preferred_element_type=F32)
        outs.append((o[:, :128] / o[:, 128:]).astype(BF16))
    return outs


def halves(width):
    return lax.broadcasted_iota(jnp.int32, (1, 8, width), 1) < 4


def to_quads(cells):
    n, _, width = cells.shape
    pairs = cells.reshape(n // 2, 2, 8, width)
    even, odd = pairs[:, 0], pairs[:, 1]
    left = jnp.where(halves(width), even, pltpu.roll(odd, 4, 1))
    right = jnp.where(halves(width), pltpu.roll(even, 4, 1), odd)
    return left, right


def from_quads(left, right):
    n, _, width = left.shape
    even = jnp.where(halves(width), left, pltpu.roll(right, 4, 1))
    odd = jnp.where(halves(width), pltpu.roll(left, 4, 1), right)
    return jnp.stack([even, odd], axis=1).reshape(2 * n, 8, width)


def window_quads(cells):
    width = cells.shape[-1]
    left, right = to_quads(cells)
    both = [side.reshape(2, QUAD, width) for side in (left, right)]
    return jnp.stack(both, axis=1)


def natural_of_quad(shape, axis):
    n = lax.broadcasted_iota(jnp.int32, shape, axis)
    u, v, r, c = (n >> 5) & 1, (n >> 4) & 1, (n >> 2) & 3, n & 3
    return (u * 4 + r) * 8 + v * 4 + c


def kernel(
    field, w_qkv, w_proj, gains, pos_bias, out,
    x, xq, wqkv, wproj, gain, bias, bias0, bias1, normed, nquad, q0, kv0, ext, q1, kv1, ctx,
    load_sem, out_sem, send_sem, recv_sem,
):
    lat, lon = lax.axis_index("lat"), lax.axis_index("lon")
    n_lat, n_lon = lax.axis_size("lat"), lax.axis_size("lon")

    def partner(dy, dx):
        return {"lat": lax.rem(lat + dy + n_lat, n_lat), "lon": lax.rem(lon + dx + n_lon, n_lon)}

    def inside(dy):
        return (lat + dy >= 0) & (lat + dy < n_lat)

    odd = lax.rem(lat, 2)
    order = (odd, 1 - odd)

    core = lax.rem(lon, 2)
    outside = 2 * core - 1

    barrier = pltpu.get_barrier_semaphore()
    for dy, dx in ((0, -1), (0, 1), (-1, 0), (1, 0), (-1, outside), (1, outside)):
        pl.when(inside(dy))(lambda: pl.semaphore_signal(
            barrier, inc=1, device_id=partner(dy, dx), device_id_type=MESH))

    loads = []

    def load(src, dst):
        copy = pltpu.make_async_copy(src, dst, load_sem.at[len(loads)])
        loads.append(copy)
        return copy

    ld_x = load(field, x)
    ld_gain = load(gains, gain)
    ld_qkv = [
        [load(w_qkv.at[s, :, pl.ds(D * c, D)], wqkv.at[s, :, pl.ds(D * c, D)]) for c in range(3)]
        for s in range(2)
    ]
    ld_bias = [load(pos_bias.at[s], bias.at[s]) for s in range(2)]
    ld_proj = [load(w_proj.at[s], wproj.at[s]) for s in range(2)]
    for copy in [ld_x, ld_gain, *ld_qkv[0], ld_bias[0], ld_proj[0]]:
        copy.start()

    ld_x.wait()
    ld_gain.wait()
    for i in range(2):
        for j in range(2):
            w = 2 * i + j
            quads = (slice(2 * i, 2 * i + 2), slice(2 * j, 2 * j + 2))
            cells = x[8 * i:8 * i + 8, 8 * j:8 * j + 8, :]
            unit = layer_norm(cells, gain[0:1, :])
            normed[w] = unit.reshape(WIN, D).astype(BF16)
            nquad[quads] = window_quads(unit).astype(BF16)
            xq[quads] = window_quads(cells)
    ld_qkv[0][0].wait()
    part = jnp.dot(nquad[...].reshape(256, D), wqkv[0, :, :D], preferred_element_type=F32) * 0.125
    q0[...] = part.astype(BF16).reshape(4, 4, QUAD, D)
    ld_qkv[0][1].wait()
    part = jnp.dot(normed[...].reshape(256, D), wqkv[0, :, D:2 * D], preferred_element_type=F32)
    kv0[:, :, :D] = part.astype(BF16).reshape(4, WIN, D)
    ld_bias[0].wait()

    def pair_bias(s, p):
        b = jnp.concatenate([bias[s, 2 * p], bias[s, 2 * p + 1]], axis=1)
        return window_quads(b.reshape(8, 8, 128)).reshape(WIN, 128)

    for p in range(PAIRS):
        bias0[p] = pair_bias(0, p)

    waves = ([], [])

    def send(wave, dy, dx, src, dst):
        n = WAVE * wave + len(waves[wave])
        copy = pltpu.make_async_remote_copy(
            src_ref=ext.at[src],
            dst_ref=ext.at[dst],
            send_sem=send_sem.at[n],
            recv_sem=recv_sem.at[n],
            device_id=partner(dy, dx),
            device_id_type=MESH,
        )
        waves[wave].append(copy)
        return copy

    for wave, i in enumerate(order):
        band = pl.ds(2 * i, 2)
        pair = pl.ds(2 * i, 2)
        if wave == 0:
            ld_qkv[0][2].wait()
            for copy in [*ld_qkv[1], ld_bias[1], ld_proj[1]]:
                copy.start()
        part = jnp.dot(
            normed[pair].reshape(128, D), wqkv[0, :, 2 * D:], preferred_element_type=F32
        )
        kv0[pair, :, D:] = part.astype(BF16).reshape(2, WIN, D)
        jobs = [(j, p) for j in range(2) for p in range(PAIRS)]
        quads = [(band, slice(2 * j, 2 * j + 2), slice(None)) for j in range(2)]
        cols = [slice(128 * p, 128 * p + 128) for p in range(PAIRS)]
        outs = attend(
            [q0[(*quads[j], cols[p])].reshape(WIN, 128) for j, p in jobs],
            [kv0[pl.ds(2 * i + j, 1), :, cols[p]].reshape(WIN, 128) for j, p in jobs],
            [kv0[pl.ds(2 * i + j, 1), :, D + 128 * p:D + 128 * p + 128].reshape(WIN, 128) for j, p in jobs],
            [bias0[p] for j, p in jobs],
        )
        for (j, p), o in zip(jobs, outs):
            ctx[(*quads[j], cols[p])] = o.reshape(2, 2, QUAD, 128)
        if wave == 0:
            ld_proj[0].wait()
        update = jnp.dot(ctx[band].reshape(128, D), wproj[0], preferred_element_type=F32)
        cells = xq[band].reshape(128, D) + update
        xq[band] = cells.reshape(2, 4, QUAD, D)
        unit = layer_norm(cells, gain[1:2, :]).astype(BF16)
        ext[pl.ds(1 + 2 * i, 2), OWN] = unit.reshape(2, 4, QUAD, D)
        if wave == 0:
            inner = (lat > 0) & (lat < n_lat - 1)
            pl.when(inner)(lambda: pl.semaphore_wait(barrier, 6))
            pl.when(jnp.logical_not(inner))(lambda: pl.semaphore_wait(barrier, 4))
        half = pl.ds(1 + 2 * i, 2)
        dy = 2 * i - 1
        here, there = pl.ds(1 + 3 * i, 1), pl.ds(5 - 5 * i, 1)
        shared, rest = pl.ds(4 - 3 * core, 1), pl.ds(1 + core, 3)
        west = send(wave, 0, -1, (half, slice(1, 2)), (half, slice(5, 6)))
        east = send(wave, 0, 1, (half, slice(4, 5)), (half, slice(0, 1)))
        first = send(wave, dy, 0, (here, shared), (there, shared))
        outward = (
            send(wave, dy, 0, (here, rest), (there, rest)),
            send(wave, dy, outside, (here, pl.ds(1 + 3 * core, 1)), (there, pl.ds(5 - 5 * core, 1))),
        )
        far = pl.ds(5 * i, 1)
        send(wave, 0, -outside, (far, shared), (far, pl.ds(5 * core, 1)))
        @pl.when(inside(dy))
        def _():
            first.start()
            outward[1].start()

        west.start()
        east.start()
        pl.when(inside(dy))(outward[0].start)

    for copy in ld_qkv[1]:
        copy.wait()
    own = ext[OWN, OWN].reshape(256, D)
    own_q = jnp.dot(own, wqkv[1, :, :D], preferred_element_type=F32) * 0.125
    q1[...] = own_q.astype(BF16).reshape(4, 4, QUAD, D)
    own_kv = jnp.dot(own, wqkv[1, :, D:], preferred_element_type=F32)
    kv1[OWN, OWN] = own_kv.astype(BF16).reshape(4, 4, QUAD, 2 * D)
    ld_bias[1].wait()
    ld_proj[1].wait()
    row = lax.broadcasted_iota(jnp.int32, (128, 128), 0)
    lane = lax.broadcasted_iota(jnp.int32, (128, 128), 1)
    key_order = (natural_of_quad((128, 128), 1) + (lane & 64) == row).astype(F32)
    for p in range(PAIRS):
        b = jnp.dot(
            pair_bias(1, p), key_order, precision=lax.Precision.HIGHEST, preferred_element_type=F32
        )
        bias1[p] = b.reshape(2, 2, QUAD, 128)

    @pl.when(lat == 0)
    def _():
        ext[0] = jnp.zeros((6, QUAD, D), BF16)

    @pl.when(lat == n_lat - 1)
    def _():
        ext[5] = jnp.zeros((6, QUAD, D), BF16)

    north = (lax.broadcasted_iota(jnp.int32, (1, 128), 1) & 63) < 32

    def shifted(group):
        qs, ks, vs, biases, places = [], [], [], [], []
        for r0, nr, u0, k0, b, closed in group:
            c0, c1 = max(2 * b - 1, 0), min(2 * b, 3) + 1
            v0, nc = c0 - (2 * b - 1), c1 - c0
            count = nr * nc * QUAD
            here = (pl.ds(k0, 2), slice(2 * b, 2 * b + 2), slice(None))
            for p in range(PAIRS):
                col = slice(128 * p, 128 * p + 128)
                place = (pl.ds(r0, nr), slice(c0, c1), slice(None), col)
                part = bias1[p:p + 1, pl.ds(u0, nr), v0:v0 + nc].reshape(count, 128)
                biases.append(part if closed is None else part + closed)
                qs.append(q1[place].reshape(count, 128))
                ks.append(kv1[(*here, col)].reshape(WIN, 128))
                vs.append(kv1[(*here, slice(D + 128 * p, D + 128 * p + 128))].reshape(WIN, 128))
                places.append((place, (nr, nc, QUAD, 128)))
        for (place, shape), o in zip(places, attend(qs, ks, vs, biases)):
            ctx[place] = o.reshape(shape)

    middle = [(1, 2, 0, 2, b, None) for b in range(3)]

    def edge(i):
        shut = jnp.where(inside(2 * i - 1), 0.0, -1e30)
        closed = jnp.where(north, jnp.where(i == 0, shut, 0.0), jnp.where(i == 1, shut, 0.0))
        return [(3 * i, 1, 1 - i, 4 * i, b, closed) for b in range(3)]

    def halo_kv(units):
        return jnp.dot(units, wqkv[1, :, D:], preferred_element_type=F32).astype(BF16)


    def finish(bands):
        block = jnp.concatenate([ctx[pl.ds(r, 1)].reshape(WIN, D) for r in bands], axis=0)
        update = jnp.dot(block, wproj[1], preferred_element_type=F32)
        for n, r in enumerate(bands):
            cells = xq[pl.ds(r, 1)].reshape(4, QUAD, D)
            cells = cells + update[WIN * n:WIN * n + WIN].reshape(4, QUAD, D)
            for j in range(2):
                left, right = [cells[2 * j + v].reshape(2, 8, D) for v in range(2)]
                out[pl.ds(4 * r, 4), 8 * j:8 * j + 8, :] = from_quads(left, right)

    def pass_on(wave):
        @pl.when(inside(2 * order[wave] - 1))
        def _():
            waves[wave][2].wait_recv()
            waves[wave][5].start()

    pass_on(0)
    shifted([middle[1]])

    def sides_arrived(wave):
        for copy in waves[wave][:2]:
            copy.wait_recv()

    def edge_arrived(wave):
        @pl.when(inside(2 * order[wave] - 1))
        def _():
            for copy in waves[wave][3:]:
                copy.wait_recv()

    def side_units(wave):
        half = pl.ds(1 + 2 * order[wave], 2)
        return [ext[half, c:c + 1].reshape(32, D) for c in (0, 5)]

    def side_kv(wave, got):
        half = pl.ds(1 + 2 * order[wave], 2)
        for n, c in enumerate((0, 5)):
            kv1[half, c:c + 1] = got[32 * n:32 * n + 32].reshape(2, 1, QUAD, 2 * D)

    sides_arrived(0)
    edge_arrived(0)
    far = 5 * order[0]
    got = halo_kv(jnp.concatenate([*side_units(0), ext[far].reshape(96, D)], axis=0))
    side_kv(0, got)
    kv1[far] = got[64:].reshape(6, QUAD, 2 * D)
    shifted(edge(order[0]))
    pass_on(1)
    sides_arrived(1)
    side_kv(1, halo_kv(jnp.concatenate(side_units(1), axis=0)))
    shifted([middle[0], middle[2]])
    finish([1, 2])
    edge_arrived(1)
    far = 5 * order[1]
    kv1[far] = halo_kv(ext[far].reshape(96, D)).reshape(6, QUAD, 2 * D)
    shifted(edge(order[1]))
    finish([0, 3])
    for wave in range(2):
        for copy in waves[wave][:2]:
            copy.wait_send()

        @pl.when(inside(2 * order[wave] - 1))
        def _():
            for copy in waves[wave][2:]:
                copy.wait_send()


def on_device(field, w_qkv, w_proj, norm_gain, pos_bias):
    rows, cols, width = field.shape
    any_space = pl.BlockSpec(memory_space=pl.ANY)
    vmem = pltpu.VMEM
    return pl.pallas_call(
        kernel,
        out_shape=jax.ShapeDtypeStruct(field.shape, F32),
        in_specs=[any_space] * 5,
        out_specs=pl.BlockSpec(memory_space=pltpu.VMEM),
        scratch_shapes=[
            vmem((rows, cols, D), F32),
            vmem((4, 4, QUAD, D), F32),
            vmem((2, D, 3 * D), BF16),
            vmem((2, D, D), BF16),
            vmem((2, D), F32),
            vmem((2, HEADS, WIN, WIN), F32),
            vmem((PAIRS, WIN, 128), F32),
            vmem((PAIRS, 2, 2, QUAD, 128), F32),
            vmem((4, WIN, D), BF16),
            vmem((4, 4, QUAD, D), BF16),
            vmem((4, 4, QUAD, D), BF16),
            vmem((4, WIN, 2 * D), BF16),
            vmem((6, 6, QUAD, D), BF16),
            vmem((4, 4, QUAD, D), BF16),
            vmem((6, 6, QUAD, 2 * D), BF16),
            vmem((4, 4, QUAD, D), BF16),
            pltpu.SemaphoreType.DMA((12,)),
            pltpu.SemaphoreType.DMA((4,)),
            pltpu.SemaphoreType.DMA((2 * WAVE,)),
            pltpu.SemaphoreType.DMA((2 * WAVE,)),
        ],
        compiler_params=pltpu.CompilerParams(
            collective_id=0, has_side_effects=True, vmem_limit_bytes=48 * 1024 * 1024
        ),
        cost_estimate=pl.CostEstimate(
            flops=3_300_000_000, bytes_accessed=13_000_000, transcendentals=400_000
        ),
        name="swin_pair",
    )(*[pltpu.with_memory_space_constraint(a, pltpu.HBM) for a in (field, w_qkv, w_proj, norm_gain, pos_bias)])


def solution(mesh):
    return jax.shard_map(
        on_device,
        mesh=mesh,
        in_specs=(P("lat", "lon", None), P(), P(), P(), P()),
        out_specs=P("lat", "lon", None),
        check_vma=False,
    )
```

```python
import functools

import jax
import jax.numpy as jnp
from jax import lax
from jax.experimental import pallas as pl
from jax.experimental.pallas import tpu as pltpu
from jax.sharding import PartitionSpec as P

D = 768
HEADS = 12
PAIRS = HEADS // 2
WIN = 64
QUAD = 16
F32 = jnp.float32
BF16 = jnp.bfloat16
MESH = pl.DeviceIdType.MESH
NT = (((1,), (1,)), ((), ()))

OWN = slice(1, 5)
WAVE = 6


def layer_norm(x, gain):
    mean = jnp.mean(x, axis=-1, keepdims=True)
    centred = x - mean
    var = jnp.mean(centred * centred, axis=-1, keepdims=True)
    return centred * lax.rsqrt(var + 1e-05) * gain


def lanes_low(shape, axis):
    return lax.broadcasted_iota(jnp.int32, shape, axis) < 64


def attend(qs, ks, vs, biases):
    low = lanes_low((1, 128), 1)
    keep0 = low.astype(F32).astype(BF16)
    keep1 = (1.0 - low.astype(F32)).astype(BF16)
    diag = (lanes_low((128, 128), 0) == lanes_low((128, 128), 1)).astype(F32).astype(BF16)
    scores = []
    for q, k, bias in zip(qs, ks, biases):
        both = jnp.concatenate([k * keep0, k * keep1], axis=0)
        scores.append(lax.dot_general(q, both, NT, preferred_element_type=F32) + bias)
    tops = []
    for s in scores:
        top0 = jnp.max(jnp.where(low, s, -jnp.inf), axis=-1, keepdims=True)
        top1 = jnp.max(jnp.where(low, -jnp.inf, s), axis=-1, keepdims=True)
        tops.append(jnp.where(low, top0, top1))
    expos = [jnp.exp(s - top).astype(BF16) for s, top in zip(scores, tops)]
    outs = []
    for e, v in zip(expos, vs):
        both = jnp.concatenate([v * keep0, v * keep1], axis=0)
        both = jnp.concatenate([both, diag], axis=1)
        o = jnp.dot(e, both, preferred_element_type=F32)
        outs.append((o[:, :128] / o[:, 128:]).astype(BF16))
    return outs


def halves(width):
    return lax.broadcasted_iota(jnp.int32, (1, 8, width), 1) < 4


def to_quads(cells):
    n, _, width = cells.shape
    pairs = cells.reshape(n // 2, 2, 8, width)
    even, odd = pairs[:, 0], pairs[:, 1]
    left = jnp.where(halves(width), even, pltpu.roll(odd, 4, 1))
    right = jnp.where(halves(width), pltpu.roll(even, 4, 1), odd)
    return left, right


def from_quads(left, right):
    n, _, width = left.shape
    even = jnp.where(halves(width), left, pltpu.roll(right, 4, 1))
    odd = jnp.where(halves(width), pltpu.roll(left, 4, 1), right)
    return jnp.stack([even, odd], axis=1).reshape(2 * n, 8, width)


def window_quads(cells):
    width = cells.shape[-1]
    left, right = to_quads(cells)
    both = [side.reshape(2, QUAD, width) for side in (left, right)]
    return jnp.stack(both, axis=1)


def natural_of_quad(shape, axis):
    n = lax.broadcasted_iota(jnp.int32, shape, axis)
    u, v, r, c = (n >> 5) & 1, (n >> 4) & 1, (n >> 2) & 3, n & 3
    return (u * 4 + r) * 8 + v * 4 + c


def kernel(
    field, w_qkv, w_proj, gains, pos_bias, out,
    x, xq, wqkv, wproj, gain, bias, bias0, bias1, normed, nquad, q0, kv0, ext, q1, kv1, ctx,
    load_sem, out_sem, send_sem, recv_sem,
):
    lat, lon = lax.axis_index("lat"), lax.axis_index("lon")
    n_lat, n_lon = lax.axis_size("lat"), lax.axis_size("lon")

    def partner(dy, dx):
        return {"lat": lax.rem(lat + dy + n_lat, n_lat), "lon": lax.rem(lon + dx + n_lon, n_lon)}

    def inside(dy):
        return (lat + dy >= 0) & (lat + dy < n_lat)

    odd = lax.rem(lat, 2)
    order = (odd, 1 - odd)

    core = lax.rem(lon, 2)
    outside = 2 * core - 1

    loads = []

    def load(src, dst):
        copy = pltpu.make_async_copy(src, dst, load_sem.at[len(loads)])
        loads.append(copy)
        return copy

    ld_x = [load(field.at[pl.ds(8 * i, 8)], x.at[pl.ds(8 * i, 8)]) for i in range(2)]
    ld_gain = load(gains, gain)
    ld_qkv = [
        [load(w_qkv.at[s, :, pl.ds(D * c, D)], wqkv.at[s, :, pl.ds(D * c, D)]) for c in range(3)]
        for s in range(2)
    ]
    ld_bias = [load(pos_bias.at[s], bias.at[s]) for s in range(2)]
    ld_proj = [load(w_proj.at[s], wproj.at[s]) for s in range(2)]
    for copy in [ld_x[0], ld_gain, ld_x[1], *ld_qkv[0], ld_bias[0], ld_proj[0]]:
        copy.start()

    barrier = pltpu.get_barrier_semaphore()
    for dy, dx in ((0, -1), (0, 1), (-1, 0), (1, 0), (-1, outside), (1, outside)):
        pl.when(inside(dy))(lambda: pl.semaphore_signal(
            barrier, inc=1, device_id=partner(dy, dx), device_id_type=MESH))

    ld_gain.wait()
    for i in range(2):
        ld_x[i].wait()
        for j in range(2):
            w = 2 * i + j
            quads = (slice(2 * i, 2 * i + 2), slice(2 * j, 2 * j + 2))
            cells = x[8 * i:8 * i + 8, 8 * j:8 * j + 8, :]
            unit = layer_norm(cells, gain[0:1, :])
            normed[w] = unit.reshape(WIN, D).astype(BF16)
            nquad[quads] = window_quads(unit).astype(BF16)
            xq[quads] = window_quads(cells)
    ld_qkv[0][0].wait()
    part = jnp.dot(nquad[...].reshape(256, D), wqkv[0, :, :D], preferred_element_type=F32) * 0.125
    q0[...] = part.astype(BF16).reshape(4, 4, QUAD, D)
    ld_qkv[0][1].wait()
    part = jnp.dot(normed[...].reshape(256, D), wqkv[0, :, D:2 * D], preferred_element_type=F32)
    kv0[:, :, :D] = part.astype(BF16).reshape(4, WIN, D)
    ld_bias[0].wait()

    def pair_bias(s, p):
        b = jnp.concatenate([bias[s, 2 * p], bias[s, 2 * p + 1]], axis=1)
        return window_quads(b.reshape(8, 8, 128)).reshape(WIN, 128)

    for p in range(PAIRS):
        bias0[p] = pair_bias(0, p)

    waves = ([], [])

    def send(wave, dy, dx, src, dst):
        n = WAVE * wave + len(waves[wave])
        copy = pltpu.make_async_remote_copy(
            src_ref=ext.at[src],
            dst_ref=ext.at[dst],
            send_sem=send_sem.at[n],
            recv_sem=recv_sem.at[n],
            device_id=partner(dy, dx),
            device_id_type=MESH,
        )
        waves[wave].append(copy)
        return copy

    for wave, i in enumerate(order):
        band = pl.ds(2 * i, 2)
        pair = pl.ds(2 * i, 2)
        if wave == 0:
            ld_qkv[0][2].wait()
        part = jnp.dot(
            normed[pair].reshape(128, D), wqkv[0, :, 2 * D:], preferred_element_type=F32
        )
        kv0[pair, :, D:] = part.astype(BF16).reshape(2, WIN, D)
        jobs = [(j, p) for j in range(2) for p in range(PAIRS)]
        quads = [(band, slice(2 * j, 2 * j + 2), slice(None)) for j in range(2)]
        cols = [slice(128 * p, 128 * p + 128) for p in range(PAIRS)]
        outs = attend(
            [q0[(*quads[j], cols[p])].reshape(WIN, 128) for j, p in jobs],
            [kv0[pl.ds(2 * i + j, 1), :, cols[p]].reshape(WIN, 128) for j, p in jobs],
            [kv0[pl.ds(2 * i + j, 1), :, D + 128 * p:D + 128 * p + 128].reshape(WIN, 128) for j, p in jobs],
            [bias0[p] for j, p in jobs],
        )
        for (j, p), o in zip(jobs, outs):
            ctx[(*quads[j], cols[p])] = o.reshape(2, 2, QUAD, 128)
        if wave == 0:
            ld_proj[0].wait()
            for copy in [*ld_qkv[1], ld_bias[1], ld_proj[1]]:
                copy.start()
        update = jnp.dot(ctx[band].reshape(128, D), wproj[0], preferred_element_type=F32)
        cells = xq[band].reshape(128, D) + update
        xq[band] = cells.reshape(2, 4, QUAD, D)
        unit = layer_norm(cells, gain[1:2, :]).astype(BF16)
        ext[pl.ds(1 + 2 * i, 2), OWN] = unit.reshape(2, 4, QUAD, D)
        if wave == 0:
            inner = (lat > 0) & (lat < n_lat - 1)
            pl.when(inner)(lambda: pl.semaphore_wait(barrier, 6))
            pl.when(jnp.logical_not(inner))(lambda: pl.semaphore_wait(barrier, 4))
        half = pl.ds(1 + 2 * i, 2)
        dy = 2 * i - 1
        here, there = pl.ds(1 + 3 * i, 1), pl.ds(5 - 5 * i, 1)
        shared, rest = pl.ds(4 - 3 * core, 1), pl.ds(1 + core, 3)
        west = send(wave, 0, -1, (half, slice(1, 2)), (half, slice(5, 6)))
        east = send(wave, 0, 1, (half, slice(4, 5)), (half, slice(0, 1)))
        first = send(wave, dy, 0, (here, shared), (there, shared))
        outward = (
            send(wave, dy, 0, (here, rest), (there, rest)),
            send(wave, dy, outside, (here, pl.ds(1 + 3 * core, 1)), (there, pl.ds(5 - 5 * core, 1))),
        )
        far = pl.ds(5 * i, 1)
        send(wave, 0, -outside, (far, shared), (far, pl.ds(5 * core, 1)))
        @pl.when(inside(dy))
        def _():
            first.start()
            outward[1].start()

        west.start()
        east.start()
        pl.when(inside(dy))(outward[0].start)

    for copy in ld_qkv[1]:
        copy.wait()
    own = ext[OWN, OWN].reshape(256, D)
    own_q = jnp.dot(own, wqkv[1, :, :D], preferred_element_type=F32) * 0.125
    q1[...] = own_q.astype(BF16).reshape(4, 4, QUAD, D)
    own_kv = jnp.dot(own, wqkv[1, :, D:], preferred_element_type=F32)
    kv1[OWN, OWN] = own_kv.astype(BF16).reshape(4, 4, QUAD, 2 * D)
    ld_bias[1].wait()
    ld_proj[1].wait()
    row = lax.broadcasted_iota(jnp.int32, (128, 128), 0)
    lane = lax.broadcasted_iota(jnp.int32, (128, 128), 1)
    key_order = (natural_of_quad((128, 128), 1) + (lane & 64) == row).astype(F32)
    for p in range(PAIRS):
        b = jnp.dot(
            pair_bias(1, p), key_order, precision=lax.Precision.HIGHEST, preferred_element_type=F32
        )
        bias1[p] = b.reshape(2, 2, QUAD, 128)

    @pl.when(lat == 0)
    def _():
        ext[0] = jnp.zeros((6, QUAD, D), BF16)

    @pl.when(lat == n_lat - 1)
    def _():
        ext[5] = jnp.zeros((6, QUAD, D), BF16)

    north = (lax.broadcasted_iota(jnp.int32, (1, 128), 1) & 63) < 32

    def shifted(group):
        qs, ks, vs, biases, places = [], [], [], [], []
        for r0, nr, u0, k0, b, closed in group:
            c0, c1 = max(2 * b - 1, 0), min(2 * b, 3) + 1
            v0, nc = c0 - (2 * b - 1), c1 - c0
            count = nr * nc * QUAD
            here = (pl.ds(k0, 2), slice(2 * b, 2 * b + 2), slice(None))
            for p in range(PAIRS):
                col = slice(128 * p, 128 * p + 128)
                place = (pl.ds(r0, nr), slice(c0, c1), slice(None), col)
                part = bias1[p:p + 1, pl.ds(u0, nr), v0:v0 + nc].reshape(count, 128)
                biases.append(part if closed is None else part + closed)
                qs.append(q1[place].reshape(count, 128))
                ks.append(kv1[(*here, col)].reshape(WIN, 128))
                vs.append(kv1[(*here, slice(D + 128 * p, D + 128 * p + 128))].reshape(WIN, 128))
                places.append((place, (nr, nc, QUAD, 128)))
        for (place, shape), o in zip(places, attend(qs, ks, vs, biases)):
            ctx[place] = o.reshape(shape)

    middle = [(1, 2, 0, 2, b, None) for b in range(3)]

    def edge(i):
        shut = jnp.where(inside(2 * i - 1), 0.0, -1e30)
        closed = jnp.where(north, jnp.where(i == 0, shut, 0.0), jnp.where(i == 1, shut, 0.0))
        return [(3 * i, 1, 1 - i, 4 * i, b, closed) for b in range(3)]

    def halo_kv(units):
        return jnp.dot(units, wqkv[1, :, D:], preferred_element_type=F32).astype(BF16)


    def finish(bands):
        block = jnp.concatenate([ctx[pl.ds(r, 1)].reshape(WIN, D) for r in bands], axis=0)
        update = jnp.dot(block, wproj[1], preferred_element_type=F32)
        for n, r in enumerate(bands):
            cells = xq[pl.ds(r, 1)].reshape(4, QUAD, D)
            cells = cells + update[WIN * n:WIN * n + WIN].reshape(4, QUAD, D)
            for j in range(2):
                left, right = [cells[2 * j + v].reshape(2, 8, D) for v in range(2)]
                out[pl.ds(4 * r, 4), 8 * j:8 * j + 8, :] = from_quads(left, right)

    def pass_on(wave):
        @pl.when(inside(2 * order[wave] - 1))
        def _():
            waves[wave][2].wait_recv()
            waves[wave][5].start()

    pass_on(0)
    shifted([middle[1]])

    def sides_arrived(wave):
        for copy in waves[wave][:2]:
            copy.wait_recv()

    def edge_arrived(wave):
        @pl.when(inside(2 * order[wave] - 1))
        def _():
            for copy in waves[wave][3:]:
                copy.wait_recv()

    def side_units(wave):
        half = pl.ds(1 + 2 * order[wave], 2)
        return [ext[half, c:c + 1].reshape(32, D) for c in (0, 5)]

    def side_kv(wave, got):
        half = pl.ds(1 + 2 * order[wave], 2)
        for n, c in enumerate((0, 5)):
            kv1[half, c:c + 1] = got[32 * n:32 * n + 32].reshape(2, 1, QUAD, 2 * D)

    sides_arrived(0)
    edge_arrived(0)
    far = 5 * order[0]
    got = halo_kv(jnp.concatenate([*side_units(0), ext[far].reshape(96, D)], axis=0))
    side_kv(0, got)
    kv1[far] = got[64:].reshape(6, QUAD, 2 * D)
    shifted(edge(order[0]))
    pass_on(1)
    sides_arrived(1)
    side_kv(1, halo_kv(jnp.concatenate(side_units(1), axis=0)))
    shifted([middle[0], middle[2]])
    finish([1, 2, 3 * order[0]])
    edge_arrived(1)
    far = 5 * order[1]
    kv1[far] = halo_kv(ext[far].reshape(96, D)).reshape(6, QUAD, 2 * D)
    shifted(edge(order[1]))
    finish([3 * order[1]])
    for wave in range(2):
        for copy in waves[wave][:2]:
            copy.wait_send()

        @pl.when(inside(2 * order[wave] - 1))
        def _():
            for copy in waves[wave][2:]:
                copy.wait_send()


def on_device(field, w_qkv, w_proj, norm_gain, pos_bias):
    rows, cols, width = field.shape
    any_space = pl.BlockSpec(memory_space=pl.ANY)
    vmem = pltpu.VMEM
    return pl.pallas_call(
        kernel,
        out_shape=jax.ShapeDtypeStruct(field.shape, F32),
        in_specs=[any_space] * 5,
        out_specs=pl.BlockSpec(memory_space=pltpu.VMEM),
        scratch_shapes=[
            vmem((rows, cols, D), F32),
            vmem((4, 4, QUAD, D), F32),
            vmem((2, D, 3 * D), BF16),
            vmem((2, D, D), BF16),
            vmem((2, D), F32),
            vmem((2, HEADS, WIN, WIN), F32),
            vmem((PAIRS, WIN, 128), F32),
            vmem((PAIRS, 2, 2, QUAD, 128), F32),
            vmem((4, WIN, D), BF16),
            vmem((4, 4, QUAD, D), BF16),
            vmem((4, 4, QUAD, D), BF16),
            vmem((4, WIN, 2 * D), BF16),
            vmem((6, 6, QUAD, D), BF16),
            vmem((4, 4, QUAD, D), BF16),
            vmem((6, 6, QUAD, 2 * D), BF16),
            vmem((4, 4, QUAD, D), BF16),
            pltpu.SemaphoreType.DMA((13,)),
            pltpu.SemaphoreType.DMA((4,)),
            pltpu.SemaphoreType.DMA((2 * WAVE,)),
            pltpu.SemaphoreType.DMA((2 * WAVE,)),
        ],
        compiler_params=pltpu.CompilerParams(
            collective_id=0, has_side_effects=True, vmem_limit_bytes=48 * 1024 * 1024
        ),
        cost_estimate=pl.CostEstimate(
            flops=3_300_000_000, bytes_accessed=13_000_000, transcendentals=400_000
        ),
        name="swin_pair",
    )(*[pltpu.with_memory_space_constraint(a, pltpu.HBM) for a in (field, w_qkv, w_proj, norm_gain, pos_bias)])


def solution(mesh):
    return jax.shard_map(
        on_device,
        mesh=mesh,
        in_specs=(P("lat", "lon", None), P(), P(), P(), P()),
        out_specs=P("lat", "lon", None),
        check_vma=False,
    )
```
